32 devices in a mesh: freq: 4 (over z), src: 8 (over y, x, core).
Axes of the slice: x: 2, y: 2, z: 4, core: 2. Of those that a mesh axis runs over, the one named last changes fastest.
Arguments:
- reflection: bfloat16 [2, 64, 1024, 1024], P(None, 'freq', None, 'src'), may hold values from -0.1875 to 0.1875
- direct_wave: float32 [1024, 64, 128], P('src', 'freq'), may hold values from -6 to 6
- first_arrival: int32 [1024, 64], P(('src', 'freq')), may hold values from 64 to 191
Outputs:
- focus_minus: float32 [1024, 64, 128], P('src', 'freq')
- focus_plus: float32 [1024, 64, 128], P('src', 'freq')
The draws below stay inside these ranges and needn't reach their ends.
All inputs are finite; a program needn't handle non-finite values.
Results may differ from the reference program's by a relative error of at most 0.035.
Values may be sent and summed in bfloat16 or wider, within the bound.
No kernel may reach another device: no remote copies, remote signals or barrier semaphores. Data moves between devices by JAX's collectives and lax.ppermute only.
A program may use at most 128 MiB of HBM per device.

```python
import math
import jax
import jax.numpy as jnp
from jax import lax

SRC_DEV = 128
NFOC = 64
NT = 512
ITERS = 2
NFREQ = 64
NX = 1024
N_SRC = 8


def touch_ends(array, key, smallest, largest):
    extent = array.shape
    index_at = [jax.random.randint(jax.random.fold_in(key, axis), (), 0, extent[axis]) for axis in range(len(extent))]
    array = array.at[tuple(index_at)].set(smallest)
    longest = extent.index(max(extent))
    index_at[longest] = (index_at[longest] + 1) % extent[longest]
    return array.at[tuple(index_at)].set(largest)


def raised(entries, rng, source, target, shards_of, factor):
    def block_of(position):
        return (jnp.arange(entries.shape[position]) // (entries.shape[position] // shards_of)).reshape((-1,) + (1,) * (entries.ndim - 1 - position))

    near = jax.random.permutation(rng, shards_of)[block_of(target)]
    other_side = (block_of(target) + shards_of // 2) % shards_of
    return jnp.where((block_of(source) == near) | (block_of(source) == other_side), factor * entries, entries)


def block_scale(stream_key, shape, shards, smallest, high):
    factor_of = 1.0
    for position, blocks in shards:
        heights = jax.random.uniform(jax.random.fold_in(jax.random.fold_in(stream_key, 6), position), (blocks,), jnp.float32, smallest / len(shards), high / len(shards))
        factor_of = factor_of * jnp.repeat(jnp.exp(heights), shape[position] // blocks).reshape((-1,) + (1,) * (len(shape) - 1 - position))
    return factor_of


def bell_draw(stream_key, dims, scale, reach, cuts=(), kind=jnp.bfloat16):
    drawn = scale * jax.random.normal(stream_key, dims, jnp.float32)
    if cuts:
        drawn = drawn * block_scale(stream_key, dims, cuts, -0.22, 0.18)
    return jnp.clip(drawn, -reach, reach).astype(kind)


def gaussian_with(stream_key, shape, scale, most, shards, heavy, kind=jnp.bfloat16):
    array = scale * jax.random.normal(stream_key, shape, jnp.float32)
    if shards:
        array = array * block_scale(stream_key, shape, shards, -0.22, 0.18)
    return jnp.clip(raised(array, jax.random.fold_in(stream_key, 3), *heavy), -most, most).astype(kind)


def setup_inputs(seed: int = 0) -> dict:
    splits = jax.random.split(jax.random.key(seed), 4)
    return {
        "reflection": gaussian_with(splits[0], (2, NFREQ, NX, NX), (2 * NX) ** -0.5, 0.1875, ((1, 4), (3, 8)), (3, 2, 8, 2.0)),
        "direct_wave": bell_draw(splits[1], (NX, NFREQ, 2 * NFOC), 1.0, 6.0, ((0, 8), (1, 4)), jnp.float32),
        "first_arrival": touch_ends(jax.random.randint(splits[2], (NX, NFOC), NT // 8, 3 * NT // 8), jax.random.fold_in(splits[2], 1), NT // 8, (3 * NT // 8) - 1).astype(jnp.int32),
    }


def transform_tables(nfreq, ntime):
    freqs = jnp.arange(1, nfreq + 1, dtype=jnp.int32)
    times = jnp.arange(ntime, dtype=jnp.int32)
    phase = ((freqs[:, None] * times[None, :]) % ntime).astype(jnp.float32) * (2.0 * math.pi / ntime)
    cosine = jnp.cos(phase)
    sine = jnp.sin(phase)
    inverse = jnp.stack([cosine * (2.0 / ntime), -sine * (2.0 / ntime)]).astype(jnp.bfloat16)
    forward = jnp.stack([cosine, -sine]).astype(jnp.bfloat16)
    return inverse, forward


def apply_window(spectrum, first_arrival, inverse, forward):
    rows_count, nfreq, width = spectrum.shape
    half = width // 2
    ntime = inverse.shape[2]
    split = spectrum.reshape(rows_count, nfreq, 2, half).astype(jnp.float32)
    signal = jnp.einsum('rfpc,pft->rct', split, inverse.astype(jnp.float32))
    times = jnp.arange(ntime, dtype=jnp.int32)
    limit = first_arrival[:, :, None]
    keep = (times[None, None, :] < limit) | (times[None, None, :] > ntime - limit)
    windowed = jnp.where(keep, signal, jnp.zeros_like(signal)).astype(jnp.bfloat16)
    back = jnp.einsum('rct,pft->rfpc', windowed.astype(jnp.float32), forward.astype(jnp.float32))
    return back.reshape(rows_count, nfreq, width).astype(jnp.float32)


def source_sum(reflection, vectors, factor):
    rounded_all = lax.optimization_barrier(vectors.astype(jnp.bfloat16))

    def one_freq(index):
        slab = lax.dynamic_index_in_dim(reflection, index, 1, keepdims=False)
        column = lax.dynamic_index_in_dim(rounded_all, index, 1, keepdims=False)
        real_rows = slab[0].astype(jnp.float32).reshape(NX, N_SRC, SRC_DEV)
        imag_rows = slab[1].astype(jnp.float32).reshape(NX, N_SRC, SRC_DEV)
        blocks = column.astype(jnp.float32).reshape(N_SRC, SRC_DEV, 2 * NFOC)
        first = jnp.einsum('rds,dsk->drk', real_rows, blocks, precision=lax.Precision.HIGHEST)
        second = jnp.einsum('rds,dsk->drk', imag_rows, blocks, precision=lax.Precision.HIGHEST)
        swapped = jnp.concatenate([-second[..., NFOC:], second[..., :NFOC]], axis=-1)
        terms = lax.optimization_barrier((first + factor * swapped).astype(jnp.bfloat16))
        return jnp.sum(terms.astype(jnp.float32), axis=0).astype(jnp.bfloat16)

    summed = lax.map(one_freq, jnp.arange(NFREQ, dtype=jnp.int32))
    return jnp.transpose(summed, (1, 0, 2))


def reference(reflection, direct_wave, first_arrival):
    inverse, forward = transform_tables(NFREQ, NT)
    focus_plus = direct_wave
    focus_minus = direct_wave
    for iteration in range(ITERS):
        spectrum = source_sum(reflection, focus_plus, 1.0)
        focus_minus = apply_window(spectrum, first_arrival, inverse, forward)
        spectrum = source_sum(reflection, focus_minus, -1.0)
        update = apply_window(spectrum, first_arrival, inverse, forward)
        focus_plus = direct_wave + update
    return focus_minus, focus_plus
```

```python
import functools
import math

import jax
import jax.numpy as jnp
import ml_dtypes
import numpy as np
from jax import lax
from jax.experimental import pallas as pl
from jax.experimental.pallas import tpu as pltpu
from jax.sharding import PartitionSpec as P

NT = 512
ITERS = 2
KEPT = 192
CHUNKS = 2
MIB = 1 << 20
BF16, F32 = jnp.bfloat16, jnp.float32


def window_tables(nfreq, chunks, groups):
    freqs = np.arange(1, nfreq + 1)
    times = np.arange(KEPT)
    phase = ((freqs[:, None] * times[None, :]) % NT).astype(np.float32) * np.float32(2.0 * math.pi / NT)
    parts = np.stack([np.cos(phase), -np.sin(phase)])
    inverse = (parts * np.float32(2.0 / NT)).astype(ml_dtypes.bfloat16)
    forward = parts.astype(ml_dtypes.bfloat16).astype(np.float32) * np.where(times == 0, 1.0, 2.0)
    forward = forward.astype(ml_dtypes.bfloat16)

    def rows(table):
        table = table.reshape(2, groups, chunks, nfreq // groups // chunks, KEPT)
        return table.transpose(0, 2, 1, 3, 4).reshape(2 * nfreq, KEPT)

    return np.ascontiguousarray(rows(inverse).T), rows(forward)


def lane_index(shape):
    return lax.broadcasted_iota(jnp.int32, shape, len(shape) - 1)


def to_chunks(by_sub, lanes):
    n = len(by_sub)
    if n == 1:
        return by_sub
    width = 64 // n
    place = (lanes % 64) // width
    result = []
    for other in range(n):
        total = None
        for a in range(n):
            shift = ((a - other) * width) % 128
            moved = pltpu.roll(by_sub[a], shift, 1) if shift else by_sub[a]
            total = moved if total is None else jnp.where(place == a, moved, total)
        result.append(total)
    return result


def pack_kernel(chunks, f_dev, rows, dw_ref, *out_refs):
    fp = f_dev // chunks
    lanes = lane_index((rows, 128))
    for b in range(fp):
        values = [dw_ref[pl.ds(a * fp + b, rows, stride=f_dev), :] for a in range(chunks)]
        for chunk, value in enumerate(to_chunks(values, lanes)):
            out_refs[chunk][b] = value
            out_refs[chunks + chunk][b] = value.astype(BF16)


def unpack_kernel(chunks, f_dev, rows, has_wave, *refs):
    fp = f_dev // chunks
    lanes = lane_index((rows, 128))
    v_refs, out_ref = refs[:chunks], refs[-1]
    for b in range(fp):
        values = [v_refs[chunk][b].astype(F32) for chunk in range(chunks)]
        for a, value in enumerate(to_chunks(values, lanes)):
            place = pl.ds(a * fp + b, rows, stride=f_dev)
            if has_wave:
                value = value + refs[chunks][place, :]
            out_ref[place, :] = value


def assemble_kernel(n_f, has_wave, where_ref, *refs):
    blocks, out_ref = refs[:n_f], refs[-1]
    rows = blocks[0].shape[1]
    for k in range(n_f):
        place = pl.ds(pl.multiple_of((where_ref[0] ^ k) * rows, rows), rows)
        value = blocks[k][...]
        if has_wave:
            value = (refs[n_f][:, place, :] + value.astype(F32)).astype(BF16)
        out_ref[:, place, :] = value


def terms_kernel(chunks, n_chip, sign, order_ref, own_ref, other_ref, v_ref, w_ref, keep_ref, send_ref):
    lanes = lane_index(v_ref.shape[1:])
    place = (lanes % 64) // (64 // chunks)
    rows = []
    for ref in (v_ref, w_ref):
        value = ref[0].astype(F32)
        turned = pltpu.roll(value, 64, 1)
        turned = jnp.where((lanes < 64) == (sign > 0), -turned, turned)
        rows += [value, turned]
    weights = [
        jnp.concatenate([jnp.where(place == a, x, 0.0) for x in rows], axis=0).astype(BF16) for a in range(chunks)
    ]
    half = n_chip // 2
    for pos in range(n_chip):
        at = order_ref[pos]
        total = None
        for a in range(chunks):
            left = jnp.concatenate(
                [own_ref[0, a, 0, at, 0], own_ref[1, a, 0, at, 0], other_ref[0, a, 0, at], other_ref[1, a, 0, at]],
                axis=1,
            )
            part = jnp.dot(left, weights[a], preferred_element_type=F32)
            total = part if total is None else total + part
        if pos < half:
            keep_ref[pos, 0] = total.astype(BF16)
        else:
            send_ref[pos - half, 0] = total.astype(BF16)


def add_kernel(*refs):
    total = refs[0][...].astype(F32)
    for ref in refs[1:-1]:
        total = total + ref[...].astype(F32)
    refs[-1][...] = total.astype(BF16)


def split_kernel(n_in, n_f, where_ref, *refs):
    rows = refs[n_in].shape[1]
    for k in range(n_f):
        place = pl.ds(pl.multiple_of((where_ref[0] ^ k) * rows, rows), rows)
        total = refs[0][0, :, place, :].astype(F32)
        for ref in refs[1:n_in]:
            total = total + ref[0, :, place, :].astype(F32)
        refs[n_in + k][...] = total.astype(BF16)


def window_kernel(chunks, n_f, tile, where_ref, limit_ref, inv_ref, fwd_ref, *refs):
    blocks, outs, (gather, scatter) = refs[:n_f], refs[n_f : 2 * n_f], refs[2 * n_f :]
    fp, rows, _ = blocks[0].shape
    depth = n_f * fp
    for k in range(n_f):
        base = (where_ref[0] ^ k) * fp
        for b in range(fp):
            gather[pl.ds(base + b, rows, stride=depth), :] = blocks[k][b].astype(F32)
    lanes = lane_index((depth, 128))
    part, place = lanes // 64, (lanes % 64) // (64 // chunks)
    times = lax.broadcasted_iota(jnp.int32, (KEPT, 128), 0)
    width = 64 // chunks
    for first in range(0, rows, tile):
        columns = []
        for r in range(first, first + tile):
            value = gather[pl.ds(r * depth, depth), :]
            spread = []
            for a in range(chunks):
                total = value
                for other in range(chunks):
                    if other != a:
                        total = jnp.where(place == other, pltpu.roll(value, ((other - a) * width) % 128, 1), total)
                spread.append(total)
            stacked = [jnp.where(part == p, x, 0.0) for p in range(2) for x in spread]
            columns.append(jnp.concatenate(stacked, axis=0).astype(BF16))
        signal = jnp.dot(inv_ref[...], jnp.concatenate(columns, axis=1), preferred_element_type=F32)
        kept = []
        for i in range(tile):
            limit = limit_ref[pl.ds(first + i, 1), :]
            kept.append(jnp.where(times < limit, signal[:, i * 128 : (i + 1) * 128], 0.0).astype(BF16))
        back = jnp.dot(fwd_ref[...], jnp.concatenate(kept, axis=1), preferred_element_type=F32)
        for i in range(tile):
            total = None
            for p in range(2):
                for a in range(chunks):
                    at = (p * chunks + a) * depth
                    piece = back[at : at + depth, i * 128 : (i + 1) * 128]
                    total = piece if total is None else jnp.where((part == p) & (place == a), piece, total)
            scatter[pl.ds((first + i) * depth, depth), :] = total
    for k in range(n_f):
        base = (where_ref[0] ^ k) * fp
        for b in range(fp):
            outs[k][b] = scatter[pl.ds(base + b, rows, stride=depth), :].astype(BF16)


def vmem():
    return pl.BlockSpec(memory_space=pltpu.VMEM)


def smem():
    return pl.BlockSpec(memory_space=pltpu.SMEM)


def params(mib):
    return pltpu.CompilerParams(vmem_limit_bytes=mib * MIB)


def cost(flops, nbytes):
    return pl.CostEstimate(flops=int(flops), bytes_accessed=int(nbytes), transcendentals=0)


def bf16(*shape):
    return jax.ShapeDtypeStruct(shape, BF16)


class Plan:
    def __init__(self, reflection, direct_wave, first_arrival):
        self.n_f, self.n_s = lax.axis_size("freq"), lax.axis_size("src")
        self.q, self.f_dev, _ = direct_wave.shape
        self.chunks = CHUNKS
        self.fp = self.f_dev // self.chunks
        self.own_rows = self.q // self.n_f
        self.n_chip = self.n_s // 2
        self.bits = self.n_chip.bit_length() - 1
        z, s = lax.axis_index("freq"), lax.axis_index("src")
        chip, self.core = s // 2, s % 2
        self.where = z.reshape(1).astype(jnp.int32)
        orders = np.zeros((2, self.n_chip), np.int32)
        for core in range(2):
            for pos in range(self.n_chip):
                for stage in range(self.bits):
                    if pos >> (self.bits - 1 - stage) & 1:
                        orders[core, pos] ^= self.mask(stage, core)
        self.order = jnp.concatenate([chip ^ jnp.asarray(orders)[self.core], self.core[None]]).astype(jnp.int32)
        inverse, forward = window_tables(self.n_f * self.f_dev, self.chunks, self.n_f)
        self.inverse, self.forward = jnp.asarray(inverse), jnp.asarray(forward)
        split = first_arrival.reshape(self.own_rows, self.chunks, 1, 64 // self.chunks)
        split = jnp.broadcast_to(split, (self.own_rows, self.chunks, 2 * self.chunks, 64 // self.chunks))
        self.limits = [split[:, i].reshape(self.own_rows, 128) for i in range(self.chunks)]
        self.reflection = reflection.reshape(2, self.chunks, self.fp, self.n_chip, 2, self.q, self.q)
        send = lax.dynamic_index_in_dim(self.reflection, 1 - self.core, 4, keepdims=False)
        self.other = self.to_core(send)

    def mask(self, stage, core):
        return 1 << ((stage + core) % self.bits)

    def to_core(self, value):
        return lax.ppermute(value, "src", [(s, s ^ 1) for s in range(self.n_s)])

    def to_chip(self, value, stage):
        pairs = [(s, s ^ (self.mask(stage, s % 2) << 1)) for s in range(self.n_s)]
        return lax.ppermute(value, "src", pairs)

    def to_group(self, value, k):
        return lax.ppermute(value, "freq", [(z, z ^ k) for z in range(self.n_f)])

    def exchange(self, blocks):
        moved = {k: self.to_group(blocks[k], k) for k in range(self.n_f - 1, 0, -1)}
        return [blocks[0]] + [moved[k] for k in range(1, self.n_f)]

    def pack(self, direct_wave):
        whole = (self.fp, self.q, 128)
        out = pl.pallas_call(
            functools.partial(pack_kernel, self.chunks, self.f_dev, self.q),
            out_shape=[jax.ShapeDtypeStruct(whole, F32)] * self.chunks + [bf16(*whole)] * self.chunks,
            in_specs=[vmem()],
            out_specs=[vmem()] * (2 * self.chunks),
            compiler_params=params(16),
            name="pack",
        )(direct_wave.reshape(self.q * self.f_dev, 128))
        return out[: self.chunks], out[self.chunks :]

    def unpack(self, values, wave=None):
        waves = [] if wave is None else [wave.reshape(self.q * self.f_dev, 128)]
        out = pl.pallas_call(
            functools.partial(unpack_kernel, self.chunks, self.f_dev, self.q, wave is not None),
            out_shape=jax.ShapeDtypeStruct((self.q * self.f_dev, 128), F32),
            in_specs=[vmem()] * (self.chunks + len(waves)),
            out_specs=vmem(),
            compiler_params=params(16),
            name="unpack",
        )(*values, *waves)
        return out.reshape(self.q, self.f_dev, 128)

    def assemble(self, blocks, wave=None):
        waves = [] if wave is None else [wave]
        return pl.pallas_call(
            functools.partial(assemble_kernel, self.n_f, wave is not None),
            out_shape=bf16(self.fp, self.q, 128),
            in_specs=[smem()] + [vmem()] * (self.n_f + len(waves)),
            out_specs=vmem(),
            compiler_params=params(8),
            cost_estimate=cost(0, MIB // 2),
            name="assemble",
        )(self.where, *blocks, *waves)

    def terms(self, vector, other_vector, sign):
        half = self.n_chip // 2
        q, fp, chunks, n_chip = self.q, self.fp, self.chunks, self.n_chip
        out = bf16(half, fp, q, 128)
        out_spec = pl.BlockSpec((half, 1, q, 128), lambda b, order: (0, b, 0, 0))
        v_spec = pl.BlockSpec((1, q, 128), lambda b, order: (b, 0, 0))
        return pl.pallas_call(
            functools.partial(terms_kernel, chunks, n_chip, sign),
            out_shape=[out, out],
            grid_spec=pltpu.PrefetchScalarGridSpec(
                num_scalar_prefetch=1,
                grid=(fp,),
                in_specs=[
                    pl.BlockSpec(
                        (2, chunks, 1, n_chip, 1, q, q), lambda b, order: (0, 0, b, 0, order[n_chip], 0, 0)
                    ),
                    pl.BlockSpec((2, chunks, 1, n_chip, q, q), lambda b, order: (0, 0, b, 0, 0, 0)),
                    v_spec,
                    v_spec,
                ],
                out_specs=[out_spec, out_spec],
            ),
            compiler_params=params(16),
            cost_estimate=cost(4 * 2 * self.f_dev * n_chip * q * q * 128, 8 * MIB),
            name="terms",
        )(self.order, self.reflection, self.other, vector, other_vector)

    def add(self, values, half):
        spec = pl.BlockSpec((half, self.fp, self.q, 128), lambda i: (1, 0, 0, 0))
        return pl.pallas_call(
            add_kernel,
            out_shape=bf16(half, self.fp, self.q, 128),
            grid=(1,),
            in_specs=[spec] * len(values),
            out_specs=pl.BlockSpec((half, self.fp, self.q, 128), lambda i: (0, 0, 0, 0)),
            compiler_params=params(16),
            cost_estimate=cost(0, MIB),
            name="add",
        )(*values)

    def split(self, values):
        spec = pl.BlockSpec((1, self.fp, self.q, 128), lambda i: (0, 0, 0, 0))
        out = bf16(self.fp, self.own_rows, 128)
        out_spec = pl.BlockSpec(out.shape, lambda i: (0, 0, 0))
        return pl.pallas_call(
            functools.partial(split_kernel, len(values), self.n_f),
            out_shape=[out] * self.n_f,
            grid=(1,),
            in_specs=[smem()] + [spec] * len(values),
            out_specs=[out_spec] * self.n_f,
            compiler_params=params(16),
            cost_estimate=cost(0, MIB),
            name="split",
        )(self.where, *values)

    def window(self, blocks, chunk):
        out = bf16(self.fp, self.own_rows, 128)
        depth = self.n_f * self.fp
        scratch = pltpu.VMEM((self.own_rows * depth, 128), F32)
        return pl.pallas_call(
            functools.partial(window_kernel, self.chunks, self.n_f, min(4, self.own_rows)),
            out_shape=[out] * self.n_f,
            in_specs=[smem()] + [vmem()] * (3 + self.n_f),
            out_specs=[vmem()] * self.n_f,
            scratch_shapes=[scratch, scratch],
            compiler_params=params(16),
            cost_estimate=cost(2e9, MIB),
            name="window",
        )(self.where, self.limits[chunk], self.inverse, self.forward, *blocks)

    def theta(self, vector, chunk, sign):
        keep, send = self.terms(vector, self.to_core(vector), sign)
        addends, half = [keep], self.n_chip // 2
        for stage in range(self.bits):
            addends.append(self.to_chip(send, stage))
            half //= 2
            if half:
                send = self.add(addends, half)
        return self.exchange(self.window(self.exchange(self.split(addends)), chunk))


def local(reflection, direct_wave, first_arrival):
    plan = Plan(reflection, direct_wave, first_arrival)
    chunks = range(plan.chunks)
    waves, plus = plan.pack(direct_wave)
    for iteration in range(ITERS):
        minus = [plan.assemble(plan.theta(plus[i], i, 1)) for i in chunks]
        last = iteration == ITERS - 1
        plus = [plan.assemble(plan.theta(minus[i], i, -1), None if last else waves[i]) for i in chunks]
    return plan.unpack(minus), plan.unpack(plus, direct_wave)


def solution(mesh):
    in_specs = (P(None, "freq", None, "src"), P("src", "freq", None), P(("src", "freq"), None))
    out_specs = (P("src", "freq", None), P("src", "freq", None))
    return jax.shard_map(local, mesh=mesh, in_specs=in_specs, out_specs=out_specs, check_vma=False)
```

```python
import functools
import math

import jax
import jax.numpy as jnp
import ml_dtypes
import numpy as np
from jax import lax
from jax.experimental import pallas as pl
from jax.experimental.pallas import tpu as pltpu
from jax.sharding import PartitionSpec as P

NT = 512
ITERS = 2
KEPT = 192
PIECES = 2
TILE = 16
MIB = 1 << 20
BF16, F32 = jnp.bfloat16, jnp.float32


def window_tables(nfreq, pieces, groups):
    freqs = np.arange(1, nfreq + 1)
    times = np.arange(KEPT)
    phase = ((freqs[:, None] * times[None, :]) % NT).astype(np.float32) * np.float32(2.0 * math.pi / NT)
    parts = np.stack([np.cos(phase), -np.sin(phase)])
    inverse = (parts * np.float32(2.0 / NT)).astype(ml_dtypes.bfloat16)
    forward = parts.astype(ml_dtypes.bfloat16).astype(np.float32) * np.where(times == 0, 1.0, 2.0)
    forward = forward.astype(ml_dtypes.bfloat16)

    def rows(table):
        table = table.reshape(2, groups, pieces, nfreq // groups // pieces, KEPT)
        return table.transpose(2, 0, 1, 3, 4).reshape(pieces, 2 * nfreq // pieces, KEPT)

    return [np.ascontiguousarray(t.T) for t in rows(inverse)], [np.ascontiguousarray(t) for t in rows(forward)]


def lane_index(shape):
    return lax.broadcasted_iota(jnp.int32, shape, len(shape) - 1)


def pack_kernel(pieces, f_dev, rows, dw_ref, arrival_ref, *refs):
    fp = f_dev // pieces
    tables, out_refs = refs[: 2 * pieces], refs[2 * pieces :]
    for piece in range(pieces):
        for b in range(fp):
            value = dw_ref[pl.ds(piece * fp + b, rows, stride=f_dev), :]
            out_refs[piece][b] = value
            out_refs[pieces + piece][b] = value.astype(BF16)
    out_refs[2 * pieces][...] = jnp.concatenate([arrival_ref[...]] * 2, axis=1)
    for table, out in zip(tables, out_refs[2 * pieces + 1 :]):
        out[...] = table[...]


def unpack_kernel(pieces, f_dev, rows, has_wave, *refs):
    fp = f_dev // pieces
    out_ref = refs[-1]
    for piece in range(pieces):
        for b in range(fp):
            value = refs[piece][b].astype(F32)
            place = pl.ds(piece * fp + b, rows, stride=f_dev)
            if has_wave:
                value = value + refs[pieces][place, :]
            out_ref[place, :] = value


def assemble_kernel(n_f, has_wave, where_ref, *refs):
    blocks, out_ref = refs[:n_f], refs[-1]
    rows = blocks[0].shape[1]
    for k in range(n_f):
        place = pl.ds(pl.multiple_of((where_ref[0] ^ k) * rows, rows), rows)
        value = blocks[k][...]
        if has_wave:
            value = (refs[n_f][:, place, :] + value.astype(F32)).astype(BF16)
        out_ref[:, place, :] = value


def half_kernel(first, core_ref, whole_ref, half_ref, sem):
    place = pl.ds(first, half_ref.shape[1])
    copy = pltpu.make_async_copy(whole_ref.at[:, place, :, core_ref[0]], half_ref, sem)
    copy.start()
    copy.wait()


def terms_kernel(n_chip, sign, order_ref, own_ref, other_ref, v_ref, w_ref, *refs):
    keep_ref, send_ref = refs[-2:]
    half = n_chip // 2
    lanes = lane_index(v_ref.shape[1:])
    for b in range(v_ref.shape[0]):
        rows = []
        for ref in (v_ref, w_ref):
            value = ref[b].astype(F32)
            turned = pltpu.roll(value, 64, 1)
            rows += [value, jnp.where((lanes < 64) == (sign > 0), -turned, turned)]
        weights = jnp.concatenate(rows, axis=0).astype(BF16)
        for pos in range(n_chip):
            at = order_ref[pos]
            left = [ref[p, b, at] for ref in (own_ref, other_ref) for p in range(2)]
            total = jnp.dot(jnp.concatenate(left, axis=1), weights, preferred_element_type=F32).astype(BF16)
            if pos < half:
                keep_ref[pos, b] = total
            else:
                send_ref[pos - half, b] = total


def add_kernel(n_in, *refs):
    out_ref = refs[-1]
    half = out_ref.shape[0]
    total = refs[0][half : 2 * half].astype(F32)
    for ref in refs[1:n_in]:
        total = total + ref[half : 2 * half].astype(F32)
    out_ref[...] = total.astype(BF16)


def split_kernel(n_in, n_f, where_ref, *refs):
    outs = refs[-n_f:]
    rows = outs[0].shape[1]
    for k in range(n_f):
        place = pl.ds(pl.multiple_of((where_ref[0] ^ k) * rows, rows), rows)
        total = refs[0][0, :, place, :].astype(F32)
        for ref in refs[1:n_in]:
            total = total + ref[0, :, place, :].astype(F32)
        outs[k][...] = total.astype(BF16)


def gather_rows(where_ref, blocks, gather):
    fp, rows, _ = blocks[0].shape
    depth = len(blocks) * fp
    for k, block in enumerate(blocks):
        base = (where_ref[0] ^ k) * fp
        for b in range(fp):
            gather[pl.ds(base + b, rows, stride=depth), :] = block[b].astype(F32)


def signal_of(inv_ref, gather, first, tile):
    depth = inv_ref.shape[1] // 2
    real = lane_index((depth, 128)) < 64
    columns = []
    for r in range(first, first + tile):
        value = gather[pl.ds(r * depth, depth), :]
        columns.append(jnp.concatenate([jnp.where(real, value, 0.0), jnp.where(real, 0.0, value)], axis=0).astype(BF16))
    return jnp.dot(inv_ref[...], jnp.concatenate(columns, axis=1), preferred_element_type=F32)


def scatter_back(fwd_ref, kept, scatter, first, tile):
    depth = fwd_ref.shape[0] // 2
    real = lane_index((depth, 128)) < 64
    back = jnp.dot(fwd_ref[...], kept, preferred_element_type=F32)
    for i in range(tile):
        columns = back[:, i * 128 : (i + 1) * 128]
        scatter[pl.ds((first + i) * depth, depth), :] = jnp.where(real, columns[:depth], columns[depth:])


def scatter_rows(where_ref, scatter, outs):
    fp, rows, _ = outs[0].shape
    depth = len(outs) * fp
    for k, out in enumerate(outs):
        base = (where_ref[0] ^ k) * fp
        for b in range(fp):
            out[b] = scatter[pl.ds(base + b, rows, stride=depth), :].astype(BF16)


def signal_kernel(n_f, tile, where_ref, inv_ref, *refs):
    blocks, (signal_ref, gather) = refs[:n_f], refs[-2:]
    gather_rows(where_ref, blocks, gather)
    for first in range(0, blocks[0].shape[1], tile):
        signal_ref[:, first * 128 : (first + tile) * 128] = signal_of(inv_ref, gather, first, tile)


def window_kernel(n_f, n_signal, tile, where_ref, limit_ref, inv_ref, fwd_ref, *refs):
    blocks, signals = refs[:n_f], refs[n_f : n_f + n_signal]
    kept_ref, outs, (gather, scatter) = refs[-n_f - 3], refs[-n_f - 2 : -2], refs[-2:]
    times = lax.broadcasted_iota(jnp.int32, (KEPT, 128), 0)
    gather_rows(where_ref, blocks, gather)
    for first in range(0, blocks[0].shape[1], tile):
        signal = signal_of(inv_ref, gather, first, tile)
        for ref in signals:
            signal = signal + ref[:, first * 128 : (first + tile) * 128]
        kept = []
        for i in range(tile):
            limit = limit_ref[pl.ds(first + i, 1), :]
            kept.append(jnp.where(times < limit, signal[:, i * 128 : (i + 1) * 128], 0.0).astype(BF16))
        kept = jnp.concatenate(kept, axis=1)
        kept_ref[:, first * 128 : (first + tile) * 128] = kept
        scatter_back(fwd_ref, kept, scatter, first, tile)
    scatter_rows(where_ref, scatter, outs)


def back_kernel(n_f, tile, where_ref, fwd_ref, kept_ref, *refs):
    outs, scatter = refs[-n_f - 1 : -1], refs[-1]
    for first in range(0, outs[0].shape[1], tile):
        scatter_back(fwd_ref, kept_ref[:, first * 128 : (first + tile) * 128], scatter, first, tile)
    scatter_rows(where_ref, scatter, outs)


def vmem():
    return pl.BlockSpec(memory_space=pltpu.VMEM)


def smem():
    return pl.BlockSpec(memory_space=pltpu.SMEM)


def anywhere():
    return pl.BlockSpec(memory_space=pl.ANY)


def bf16(*shape):
    return jax.ShapeDtypeStruct(shape, BF16)


def call(kernel, name, outs, scalars, values, after=(), scratch=(), mib=12, weight=2e10):
    return pl.pallas_call(
        kernel,
        out_shape=outs,
        in_specs=[smem()] * len(scalars) + [vmem()] * len(values) + [anywhere()] * len(after),
        out_specs=[vmem()] * len(outs),
        scratch_shapes=list(scratch),
        compiler_params=pltpu.CompilerParams(vmem_limit_bytes=mib * MIB),
        cost_estimate=pl.CostEstimate(flops=int(weight), bytes_accessed=MIB, transcendentals=0),
        name=name,
    )(*scalars, *values, *after)


class Plan:
    def __init__(self, reflection, direct_wave, first_arrival):
        self.n_f, self.n_s = lax.axis_size("freq"), lax.axis_size("src")
        self.q, self.f_dev, _ = direct_wave.shape
        self.pieces = PIECES
        self.fp = self.f_dev // self.pieces
        self.own_rows = self.q // self.n_f
        self.tile = min(TILE, self.own_rows)
        self.n_chip = self.n_s // 2
        self.bits = self.n_chip.bit_length() - 1
        z, s = lax.axis_index("freq"), lax.axis_index("src")
        chip, core = s // 2, s % 2
        self.where = z.reshape(1).astype(jnp.int32)
        orders = np.zeros((2, self.n_chip), np.int32)
        for c in range(2):
            for pos in range(self.n_chip):
                for stage in range(self.bits):
                    if pos >> (self.bits - 1 - stage) & 1:
                        orders[c, pos] ^= self.mask(stage, c)
        self.order = (chip ^ jnp.asarray(orders)[core]).astype(jnp.int32)
        self.whole = (self.fp, self.q, 128)
        reflection = reflection.reshape(2, self.f_dev, self.n_chip, 2, self.q, self.q)
        self.other = [self.to_core(self.half(reflection, 1 - core, i)) for i in range(self.pieces)]
        self.own = [self.half(reflection, core, i) for i in range(self.pieces)]
        self.pack(direct_wave, first_arrival)

    def mask(self, stage, core):
        return 1 << ((stage + core) % self.bits)

    def to_core(self, value):
        return lax.ppermute(value, "src", [(s, s ^ 1) for s in range(self.n_s)])

    def to_chip(self, value, stage):
        pairs = [(s, s ^ (self.mask(stage, s % 2) << 1)) for s in range(self.n_s)]
        return lax.ppermute(value, "src", pairs)

    def exchange(self, blocks):
        pairs = {k: [(z, z ^ k) for z in range(self.n_f)] for k in range(self.n_f)}
        moved = {k: lax.ppermute(blocks[k], "freq", pairs[k]) for k in range(self.n_f - 1, 0, -1)}
        return [blocks[0]] + [moved[k] for k in range(1, self.n_f)]

    def half(self, reflection, core, piece):
        return pl.pallas_call(
            functools.partial(half_kernel, piece * self.fp),
            out_shape=bf16(2, self.fp, self.n_chip, self.q, self.q),
            in_specs=[smem(), pl.BlockSpec(memory_space=pltpu.HBM)],
            out_specs=vmem(),
            scratch_shapes=[pltpu.SemaphoreType.DMA],
            compiler_params=pltpu.CompilerParams(vmem_limit_bytes=58 * MIB),
            name="half",
        )(core.reshape(1), reflection)

    def pack(self, direct_wave, first_arrival):
        n = self.pieces
        inverse, forward = window_tables(self.n_f * self.f_dev, n, self.n_f)
        tables = [jnp.asarray(t) for t in inverse + forward]
        limit = jax.ShapeDtypeStruct((self.own_rows, 128), jnp.int32)
        outs = [jax.ShapeDtypeStruct(self.whole, F32)] * n + [bf16(*self.whole)] * n + [limit]
        out = call(
            functools.partial(pack_kernel, n, self.f_dev, self.q),
            "pack",
            outs + [bf16(*t.shape) for t in tables],
            [],
            [direct_wave.reshape(self.q * self.f_dev, 128), first_arrival, *tables],
        )
        self.waves, self.start, self.limit = out[:n], out[n : 2 * n], out[2 * n]
        self.inverse, self.forward = out[2 * n + 1 : 3 * n + 1], out[3 * n + 1 :]

    def unpack(self, values, wave=None):
        waves = [] if wave is None else [wave.reshape(self.q * self.f_dev, 128)]
        out = call(
            functools.partial(unpack_kernel, self.pieces, self.f_dev, self.q, wave is not None),
            "unpack",
            [jax.ShapeDtypeStruct((self.q * self.f_dev, 128), F32)],
            [],
            [*values, *waves],
        )
        return out[0].reshape(self.q, self.f_dev, 128)

    def assemble(self, blocks, wave, after):
        waves = [] if wave is None else [wave]
        kernel = functools.partial(assemble_kernel, self.n_f, wave is not None)
        return call(kernel, "assemble", [bf16(*self.whole)], [self.where], [*blocks, *waves], after)[0]

    def terms(self, piece, vector, other_vector, sign, after):
        out = bf16(self.n_chip // 2, *self.whole)
        kernel = functools.partial(terms_kernel, self.n_chip, sign)
        values = [self.own[piece], self.other[piece], vector, other_vector]
        return call(kernel, "terms", [out, out], [self.order], values, after, mib=20)

    def add(self, values, after):
        out = bf16(values[-1].shape[0] // 2, *self.whole)
        return call(functools.partial(add_kernel, len(values)), "add", [out], [], values, after)[0]

    def split(self, values, after):
        outs = [bf16(self.fp, self.own_rows, 128)] * self.n_f
        kernel = functools.partial(split_kernel, len(values), self.n_f)
        return call(kernel, "split", outs, [self.where], values, after)

    def rows_scratch(self):
        return pltpu.VMEM((self.own_rows * self.n_f * self.fp, 128), F32)

    def signal(self, piece, blocks, after):
        out = jax.ShapeDtypeStruct((KEPT, self.own_rows * 128), F32)
        kernel = functools.partial(signal_kernel, self.n_f, self.tile)
        values = [self.inverse[piece], *blocks]
        return call(kernel, "signal", [out], [self.where], values, after, [self.rows_scratch()], 20)[0]

    def window(self, piece, back, blocks, signals, after):
        outs = [bf16(KEPT, self.own_rows * 128)] + [bf16(self.fp, self.own_rows, 128)] * self.n_f
        kernel = functools.partial(window_kernel, self.n_f, len(signals), self.tile)
        values = [self.limit, self.inverse[piece], self.forward[back], *blocks, *signals]
        scratch = [self.rows_scratch(), self.rows_scratch()]
        kept, *blocks = call(kernel, "window", outs, [self.where], values, after, scratch, 20)
        return kept, blocks

    def back(self, piece, kept, after):
        outs = [bf16(self.fp, self.own_rows, 128)] * self.n_f
        kernel = functools.partial(back_kernel, self.n_f, self.tile)
        values = [self.forward[piece], kept]
        return call(kernel, "back", outs, [self.where], values, after, [self.rows_scratch()], 20)

    def theta(self, vectors, sign, waves, after):
        pieces = range(self.pieces)
        held, addends = [], []
        for i in pieces:
            vector = vectors(i, after)
            keep, send = self.terms(i, vector, self.to_core(vector), sign, after if i == 0 else [send])
            held.append(vector)
            addends.append([keep, self.to_chip(send, 0)])
        after = [send]
        for stage in range(1, self.bits):
            for i in pieces:
                send = self.add(addends[i], after)
                addends[i].append(self.to_chip(send, stage))
                after = [send]
        blocks = []
        for i in pieces:
            sums = self.split(addends[i], after)
            blocks.append(self.exchange(sums))
            after = [sums[0]]
        signals = []
        for i in pieces[:-1]:
            signals.append(self.signal(i, blocks[i], after))
            after = [signals[-1]]
        kept, out = self.window(self.pieces - 1, 0, blocks[-1], signals, after)
        arrived, after = [self.exchange(out)], [out[0]]
        for i in pieces[1:]:
            out = self.back(i, kept, after)
            arrived.append(self.exchange(out))
            after = [out[0]]
        return held, lambda i, then: self.assemble(arrived[i], waves and waves[i], after if i == 0 else then), after


def local(reflection, direct_wave, first_arrival):
    plan = Plan(reflection, direct_wave, first_arrival)
    vectors, after = lambda i, then: plan.start[i], []
    for step in range(2 * ITERS):
        waves = plan.waves if step % 2 == 1 and step < 2 * ITERS - 1 else None
        held, vectors, after = plan.theta(vectors, 1 if step % 2 == 0 else -1, waves, after)
    return plan.unpack(held), plan.unpack([vectors(i, after) for i in range(plan.pieces)], direct_wave)


def solution(mesh):
    in_specs = (P(None, "freq", None, "src"), P("src", "freq", None), P(("src", "freq"), None))
    out_specs = (P("src", "freq", None), P("src", "freq", None))
    return jax.shard_map(local, mesh=mesh, in_specs=in_specs, out_specs=out_specs, check_vma=False)
```

```python
import functools
import math

import jax
import jax.numpy as jnp
import ml_dtypes
import numpy as np
from jax import lax
from jax.experimental import pallas as pl
from jax.experimental.pallas import tpu as pltpu
from jax.sharding import PartitionSpec as P

NT = 512
ITERS = 2
KEPT = 192
CHUNKS = 2
MIB = 1 << 20
WEIGHT = 3e9
BYTES = MIB
TILE = 16
PAD = 4
TERMS_MIB = 32
OTHER_MIB = 12
BF16, F32 = jnp.bfloat16, jnp.float32


def window_tables(nfreq, chunks, groups):
    freqs = np.arange(1, nfreq + 1)
    times = np.arange(KEPT)
    phase = ((freqs[:, None] * times[None, :]) % NT).astype(np.float32) * np.float32(2.0 * math.pi / NT)
    parts = np.stack([np.cos(phase), -np.sin(phase)])
    inverse = (parts * np.float32(2.0 / NT)).astype(ml_dtypes.bfloat16)
    forward = parts.astype(ml_dtypes.bfloat16).astype(np.float32) * np.where(times == 0, 1.0, 2.0)
    forward = forward.astype(ml_dtypes.bfloat16)

    def rows(table):
        table = table.reshape(2, groups, chunks, nfreq // groups // chunks, KEPT)
        return table.transpose(0, 2, 1, 3, 4).reshape(2 * nfreq, KEPT)

    return np.ascontiguousarray(rows(inverse).T), rows(forward)


def lane_index(shape):
    return lax.broadcasted_iota(jnp.int32, shape, len(shape) - 1)


def to_chunks(by_sub, lanes):
    n = len(by_sub)
    if n == 1:
        return by_sub
    width = 64 // n
    place = (lanes % 64) // width
    result = []
    for other in range(n):
        total = None
        for a in range(n):
            shift = ((a - other) * width) % 128
            moved = pltpu.roll(by_sub[a], shift, 1) if shift else by_sub[a]
            total = moved if total is None else jnp.where(place == a, moved, total)
        result.append(total)
    return result


def pack_kernel(chunks, f_dev, rows, dw_ref, *out_refs):
    fp = f_dev // chunks
    lanes = lane_index((rows, 128))
    for b in range(fp):
        values = [dw_ref[pl.ds(a * fp + b, rows, stride=f_dev), :] for a in range(chunks)]
        for out_ref, value in zip(out_refs, to_chunks(values, lanes)):
            out_ref[b] = value.astype(BF16)


def limits_kernel(chunks, arrival_ref, *refs):
    width = 64 // chunks
    for chunk, out_ref in enumerate(refs[-chunks:]):
        limit = arrival_ref[:, chunk * width : (chunk + 1) * width]
        out_ref[...] = jnp.concatenate([limit] * (2 * chunks), axis=1)


def wave_kernel(chunks, f_dev, rows, dw_ref, *refs):
    fp = f_dev // chunks
    lanes = lane_index((rows, 128))
    for b in range(fp):
        values = [dw_ref[pl.ds(a * fp + b, rows, stride=f_dev), :] for a in range(chunks)]
        for out_ref, value in zip(refs[-chunks:], to_chunks(values, lanes)):
            out_ref[b] = value


def unpack_kernel(chunks, f_dev, rows, has_wave, *refs):
    fp = f_dev // chunks
    lanes = lane_index((rows, 128))
    v_refs, out_ref = refs[:chunks], refs[-1]
    for b in range(fp):
        values = [v_refs[chunk][b].astype(F32) for chunk in range(chunks)]
        for a, value in enumerate(to_chunks(values, lanes)):
            place = pl.ds(a * fp + b, rows, stride=f_dev)
            if has_wave:
                value = value + refs[chunks][place, :]
            out_ref[place, :] = value


def assemble_kernel(n_f, has_wave, where_ref, *refs):
    blocks, out_ref = refs[:n_f], refs[-1]
    rows = blocks[0].shape[1]
    for k in range(n_f):
        place = pl.ds(pl.multiple_of((where_ref[0] ^ k) * rows, rows), rows)
        value = blocks[k][...]
        if has_wave:
            value = (refs[n_f][:, place, :] + value.astype(F32)).astype(BF16)
        out_ref[:, place, :] = value


def terms_kernel(chunks, sign, places_ref, whole_ref, v_ref, *refs):
    out_ref = refs[-1]
    lanes = lane_index(v_ref.shape[1:])
    place = (lanes % 64) // (64 // chunks)
    for b in range(v_ref.shape[0]):
        value = v_ref[b].astype(F32)
        turned = pltpu.roll(value, 64, 1)
        turned = jnp.where((lanes < 64) == (sign > 0), -turned, turned)
        weights = [jnp.where(place == a, x, 0.0) for a in range(chunks) for x in (value, turned)]
        weights = jnp.concatenate(weights, axis=0).astype(BF16)
        for pos in range(out_ref.shape[0]):
            at = places_ref[pos]
            left = [whole_ref[p, a, b, at] for a in range(chunks) for p in range(2)]
            total = jnp.dot(jnp.concatenate(left, axis=1), weights, preferred_element_type=F32)
            out_ref[pos, b] = total.astype(BF16)


def add_kernel(n_in, *refs):
    out_ref = refs[-1]
    half = out_ref.shape[0]
    total = refs[0][half : 2 * half].astype(F32)
    for ref in refs[1:n_in]:
        total = total + ref[half : 2 * half].astype(F32)
    out_ref[...] = total.astype(BF16)


def split_kernel(n_in, n_f, where_ref, *refs):
    outs = refs[-n_f:]
    rows = outs[0].shape[1]
    for k in range(n_f):
        place = pl.ds(pl.multiple_of((where_ref[0] ^ k) * rows, rows), rows)
        total = refs[0][0, :, place, :].astype(F32)
        for ref in refs[1:n_in]:
            total = total + ref[0, :, place, :].astype(F32)
        outs[k][...] = total.astype(BF16)


def window_kernel(chunks, n_f, tile, where_ref, limit_ref, inv_ref, fwd_ref, *refs):
    blocks, outs, (gather, scatter) = refs[:n_f], refs[-n_f - 2 : -2], refs[-2:]
    fp, rows, _ = blocks[0].shape
    depth = n_f * fp
    step = depth + PAD
    for k in range(n_f):
        base = (where_ref[0] ^ k) * fp
        for b in range(fp):
            gather[pl.ds(base + b, rows, stride=step), :] = blocks[k][b].astype(F32)
    lanes = lane_index((depth, 128))
    part, place = lanes // 64, (lanes % 64) // (64 // chunks)
    times = lax.broadcasted_iota(jnp.int32, (KEPT, 128), 0)
    width = 64 // chunks
    for first in range(0, rows, tile):
        columns = []
        for r in range(first, first + tile):
            value = gather[pl.ds(r * step, depth), :]
            spread = []
            for a in range(chunks):
                total = value
                for other in range(chunks):
                    if other != a:
                        total = jnp.where(place == other, pltpu.roll(value, ((other - a) * width) % 128, 1), total)
                spread.append(total)
            stacked = [jnp.where(part == p, x, 0.0) for p in range(2) for x in spread]
            columns.append(jnp.concatenate(stacked, axis=0).astype(BF16))
        signal = jnp.dot(inv_ref[...], jnp.concatenate(columns, axis=1), preferred_element_type=F32)
        kept = []
        for i in range(tile):
            limit = limit_ref[pl.ds(first + i, 1), :]
            kept.append(jnp.where(times < limit, signal[:, i * 128 : (i + 1) * 128], 0.0).astype(BF16))
        back = jnp.dot(fwd_ref[...], jnp.concatenate(kept, axis=1), preferred_element_type=F32)
        for i in range(tile):
            total = None
            for p in range(2):
                for a in range(chunks):
                    at = (p * chunks + a) * depth
                    piece = back[at : at + depth, i * 128 : (i + 1) * 128]
                    total = piece if total is None else jnp.where((part == p) & (place == a), piece, total)
            scatter[pl.ds((first + i) * step, depth), :] = total
    for k in range(n_f):
        base = (where_ref[0] ^ k) * fp
        for b in range(fp):
            outs[k][b] = scatter[pl.ds(base + b, rows, stride=step), :].astype(BF16)


def vmem():
    return pl.BlockSpec(memory_space=pltpu.VMEM)


def anywhere():
    return pl.BlockSpec(memory_space=pl.ANY)


def smem():
    return pl.BlockSpec(memory_space=pltpu.SMEM)


def params(mib):
    return pltpu.CompilerParams(vmem_limit_bytes=mib * MIB)


def cost(flops, nbytes):
    return pl.CostEstimate(flops=int(flops), bytes_accessed=int(nbytes), transcendentals=0)


def bf16(*shape):
    return jax.ShapeDtypeStruct(shape, BF16)


class Plan:
    def __init__(self, reflection, direct_wave):
        self.n_f, self.n_s = lax.axis_size("freq"), lax.axis_size("src")
        self.q, self.f_dev, _ = direct_wave.shape
        self.chunks = CHUNKS
        self.fp = self.f_dev // self.chunks
        self.own_rows = self.q // self.n_f
        self.n_chip = self.n_s // 2
        self.bits = self.n_chip.bit_length() - 1
        z, s = lax.axis_index("freq"), lax.axis_index("src")
        chip, self.core = s // 2, s % 2
        self.where = z.reshape(1).astype(jnp.int32)
        orders = np.zeros((2, self.n_chip), np.int32)
        for core in range(2):
            for pos in range(self.n_chip):
                for stage in range(self.bits):
                    if pos >> (self.bits - 1 - stage) & 1:
                        orders[core, pos] ^= self.mask(stage, core)
        orders = jnp.asarray(orders)
        self.near = ((chip ^ orders[self.core]) * 2 + self.core).astype(jnp.int32)
        self.far = ((chip ^ orders[1 - self.core]) * 2 + 1 - self.core).astype(jnp.int32)
        inverse, forward = window_tables(self.n_f * self.f_dev, self.chunks, self.n_f)
        self.tables = [jnp.asarray(inverse), jnp.asarray(forward)]
        self.reflection = reflection.reshape(2, self.chunks, self.fp, self.n_s, self.q, self.q)

    def mask(self, stage, core):
        return 1 << ((stage + core) % self.bits)

    def to_core(self, value):
        return lax.ppermute(value, "src", [(s, s ^ 1) for s in range(self.n_s)])

    def to_chip(self, value, stage):
        pairs = [(s, s ^ (self.mask(stage, s % 2) << 1)) for s in range(self.n_s)]
        return lax.ppermute(value, "src", pairs)

    def to_group(self, value, k):
        return lax.ppermute(value, "freq", [(z, z ^ k) for z in range(self.n_f)])

    def exchange(self, blocks):
        moved = {k: self.to_group(blocks[k], k) for k in range(self.n_f - 1, 0, -1)}
        return [blocks[0]] + [moved[k] for k in range(1, self.n_f)]

    def pack(self, direct_wave):
        return pl.pallas_call(
            functools.partial(pack_kernel, self.chunks, self.f_dev, self.q),
            out_shape=[bf16(self.fp, self.q, 128)] * self.chunks,
            in_specs=[vmem()],
            out_specs=[vmem()] * self.chunks,
            compiler_params=params(OTHER_MIB),
            cost_estimate=cost(WEIGHT, BYTES),
            name="pack",
        )(direct_wave.reshape(self.q * self.f_dev, 128))

    def make_limits(self, first_arrival, after):
        self.limits = pl.pallas_call(
            functools.partial(limits_kernel, self.chunks),
            out_shape=[jax.ShapeDtypeStruct((self.own_rows, 128), jnp.int32)] * self.chunks,
            in_specs=[vmem()] + [anywhere()] * len(after),
            out_specs=[vmem()] * self.chunks,
            compiler_params=params(OTHER_MIB),
            cost_estimate=cost(WEIGHT, BYTES),
            name="limits",
        )(first_arrival, *after)
        return self.limits[:1]

    def waves(self, direct_wave, after):
        n = self.chunks
        return pl.pallas_call(
            functools.partial(wave_kernel, n, self.f_dev, self.q),
            out_shape=[jax.ShapeDtypeStruct((self.fp, self.q, 128), F32)] * n,
            in_specs=[vmem()] + [anywhere()] * len(after),
            out_specs=[vmem()] * n,
            compiler_params=params(OTHER_MIB),
            name="wave",
        )(direct_wave.reshape(self.q * self.f_dev, 128), *after)

    def unpack(self, values, wave=None):
        waves = [] if wave is None else [wave.reshape(self.q * self.f_dev, 128)]
        out = pl.pallas_call(
            functools.partial(unpack_kernel, self.chunks, self.f_dev, self.q, wave is not None),
            out_shape=jax.ShapeDtypeStruct((self.q * self.f_dev, 128), F32),
            in_specs=[vmem()] * (self.chunks + len(waves)),
            out_specs=vmem(),
            compiler_params=params(OTHER_MIB),
            name="unpack",
        )(*values, *waves)
        return out.reshape(self.q, self.f_dev, 128)

    def assemble(self, blocks, wave, after):
        waves = [] if wave is None else [wave]
        return pl.pallas_call(
            functools.partial(assemble_kernel, self.n_f, wave is not None),
            out_shape=bf16(self.fp, self.q, 128),
            in_specs=[smem()] + [vmem()] * (self.n_f + len(waves)) + [anywhere()] * len(after),
            out_specs=vmem(),
            compiler_params=params(OTHER_MIB),
            cost_estimate=cost(WEIGHT, BYTES),
            name="assemble",
        )(self.where, *blocks, *waves, *after)

    def terms(self, vector, places, sign, after):
        return pl.pallas_call(
            functools.partial(terms_kernel, self.chunks, sign),
            out_shape=bf16(self.n_chip, self.fp, self.q, 128),
            in_specs=[smem()] + [vmem()] * 2 + [anywhere()] * len(after),
            out_specs=vmem(),
            compiler_params=params(TERMS_MIB),
            cost_estimate=cost(WEIGHT, BYTES),
            name="terms",
        )(places, self.reflection, vector, *after)

    def add(self, values, half, after):
        return pl.pallas_call(
            functools.partial(add_kernel, len(values)),
            out_shape=bf16(half, self.fp, self.q, 128),
            in_specs=[vmem()] * len(values) + [anywhere()] * len(after),
            out_specs=vmem(),
            compiler_params=params(OTHER_MIB),
            cost_estimate=cost(WEIGHT, BYTES),
            name="add",
        )(*values, *after)

    def split(self, values, after):
        out = bf16(self.fp, self.own_rows, 128)
        return pl.pallas_call(
            functools.partial(split_kernel, len(values), self.n_f),
            out_shape=[out] * self.n_f,
            in_specs=[smem()] + [vmem()] * len(values) + [anywhere()] * len(after),
            out_specs=[vmem()] * self.n_f,
            compiler_params=params(OTHER_MIB),
            cost_estimate=cost(WEIGHT, BYTES),
            name="split",
        )(self.where, *values, *after)

    def window(self, blocks, chunk, after):
        out = bf16(self.fp, self.own_rows, 128)
        depth = self.n_f * self.fp + PAD
        scratch = pltpu.VMEM((self.own_rows * depth, 128), F32)
        return pl.pallas_call(
            functools.partial(window_kernel, self.chunks, self.n_f, min(TILE, self.own_rows)),
            out_shape=[out] * self.n_f,
            in_specs=[smem()] + [vmem()] * (3 + self.n_f) + [anywhere()] * len(after),
            out_specs=[vmem()] * self.n_f,
            scratch_shapes=[scratch, scratch],
            compiler_params=params(OTHER_MIB),
            cost_estimate=cost(WEIGHT, BYTES),
            name="window",
        )(self.where, self.limits[chunk], *self.tables, *blocks, *after)


class Chain:
    def __init__(self, plan, chunk, vector):
        self.plan, self.chunk, self.wave = plan, chunk, None
        self.vector, self.done, self.minus = vector, 0, None
        self.todo = self.theta()

    def theta(self):
        return [self.far, self.near] + [self.add] * self.plan.bits + [self.split, self.window, self.assemble]

    def step(self, after):
        return self.todo.pop(0)(after)

    def sign(self):
        return 1 if self.done % 2 == 0 else -1

    def far(self, after):
        out = self.plan.terms(self.vector, self.plan.far, self.sign(), after)
        self.arriving = self.plan.to_core(out)
        return [out]

    def near(self, after):
        out = self.plan.terms(self.vector, self.plan.near, self.sign(), after)
        self.addends, self.half = [out, self.arriving], self.plan.n_chip
        return [out]

    def add(self, after):
        plan = self.plan
        self.half //= 2
        send = plan.add(self.addends, self.half, after)
        self.addends.append(plan.to_chip(send, len(self.addends) - 2))
        return [send]

    def split(self, after):
        blocks = self.plan.split(self.addends, after)
        self.blocks = self.plan.exchange(blocks)
        return [blocks[0]]

    def window(self, after):
        blocks = self.plan.window(self.blocks, self.chunk, after)
        self.blocks = self.plan.exchange(blocks)
        return [blocks[0]]

    def assemble(self, after):
        self.done += 1
        wave = self.wave if self.done % 2 == 0 and self.done < 2 * ITERS else None
        self.vector = self.plan.assemble(self.blocks, wave, after)
        if self.done == 2 * ITERS - 1:
            self.minus = self.vector
        self.todo = self.theta()
        return [self.vector]


def local(reflection, direct_wave, first_arrival):
    plan = Plan(reflection, direct_wave)
    plus = plan.pack(direct_wave)
    chains = [Chain(plan, i, plus[i]) for i in range(plan.chunks)]
    first, second = chains[0], chains[-1]
    after = []
    for step in range(2 * ITERS):
        for place, chain in enumerate([first, first, second, first, second, second]):
            if step and place in (0, 2):
                after = chain.step(after)
            after = chain.step(after)
        if step == 0:
            after = plan.make_limits(first_arrival, after)
        if step == 1:
            waves = plan.waves(direct_wave, after)
            after = waves[:1]
            for chain, wave in zip(chains, waves):
                chain.wave = wave
        for _ in range(1 + plan.bits):
            for chain in chains:
                after = chain.step(after)
    for chain in chains:
        after = chain.step(after)
    return plan.unpack([c.minus for c in chains]), plan.unpack([c.vector for c in chains], direct_wave)


def solution(mesh):
    in_specs = (P(None, "freq", None, "src"), P("src", "freq", None), P(("src", "freq"), None))
    out_specs = (P("src", "freq", None), P("src", "freq", None))
    return jax.shard_map(local, mesh=mesh, in_specs=in_specs, out_specs=out_specs, check_vma=False)
```

```python
import functools
import math

import jax
import jax.numpy as jnp
import ml_dtypes
import numpy as np
from jax import lax
from jax.experimental import pallas as pl
from jax.experimental.pallas import tpu as pltpu
from jax.sharding import PartitionSpec as P

NT = 512
ITERS = 2
KEPT = 192
CHUNKS = 2
MIB = 1 << 20
WEIGHT = 3e9
UNROLL = 8
BYTES = MIB
TILE = 16
PAD = 4
TERMS_MIB = 32
OTHER_MIB = 12
BF16, F32 = jnp.bfloat16, jnp.float32


def window_tables(nfreq, chunks, groups):
    freqs = np.arange(1, nfreq + 1)
    times = np.arange(KEPT)
    phase = ((freqs[:, None] * times[None, :]) % NT).astype(np.float32) * np.float32(2.0 * math.pi / NT)
    parts = np.stack([np.cos(phase), -np.sin(phase)])
    inverse = (parts * np.float32(2.0 / NT)).astype(ml_dtypes.bfloat16)
    forward = parts.astype(ml_dtypes.bfloat16).astype(np.float32) * np.where(times == 0, 1.0, 2.0)
    forward = forward.astype(ml_dtypes.bfloat16)

    def rows(table):
        table = table.reshape(2, groups, chunks, nfreq // groups // chunks, KEPT)
        return table.transpose(0, 2, 1, 3, 4).reshape(2 * nfreq, KEPT)

    return np.ascontiguousarray(rows(inverse).T), rows(forward)


def lane_index(shape):
    return lax.broadcasted_iota(jnp.int32, shape, len(shape) - 1)


def to_chunks(by_sub, lanes):
    n = len(by_sub)
    if n == 1:
        return by_sub
    width = 64 // n
    place = (lanes % 64) // width
    result = []
    for other in range(n):
        total = None
        for a in range(n):
            shift = ((a - other) * width) % 128
            moved = pltpu.roll(by_sub[a], shift, 1) if shift else by_sub[a]
            total = moved if total is None else jnp.where(place == a, moved, total)
        result.append(total)
    return result


def pack_kernel(chunks, f_dev, rows, dw_ref, *out_refs):
    fp = f_dev // chunks
    lanes = lane_index((rows, 128))

    @pl.loop(0, fp)
    def _(b):
        values = [dw_ref[pl.ds(a * fp + b, rows, stride=f_dev), :] for a in range(chunks)]
        for out_ref, value in zip(out_refs, to_chunks(values, lanes)):
            out_ref[b] = value.astype(BF16)


def limits_kernel(chunks, arrival_ref, *refs):
    width = 64 // chunks
    for chunk, out_ref in enumerate(refs[-chunks:]):
        limit = arrival_ref[:, chunk * width : (chunk + 1) * width]
        out_ref[...] = jnp.concatenate([limit] * (2 * chunks), axis=1)


def wave_kernel(chunks, f_dev, rows, dw_ref, *refs):
    fp = f_dev // chunks
    lanes = lane_index((rows, 128))

    @pl.loop(0, fp)
    def _(b):
        values = [dw_ref[pl.ds(a * fp + b, rows, stride=f_dev), :] for a in range(chunks)]
        for out_ref, value in zip(refs[-chunks:], to_chunks(values, lanes)):
            out_ref[b] = value


def unpack_kernel(chunks, f_dev, rows, has_wave, *refs):
    fp = f_dev // chunks
    lanes = lane_index((rows, 128))
    v_refs, out_ref = refs[:chunks], refs[-1]
    for b in range(fp):
        values = [v_refs[chunk][b].astype(F32) for chunk in range(chunks)]
        for a, value in enumerate(to_chunks(values, lanes)):
            place = pl.ds(a * fp + b, rows, stride=f_dev)
            if has_wave:
                value = value + refs[chunks][place, :]
            out_ref[place, :] = value


def assemble_kernel(n_f, has_wave, where_ref, *refs):
    blocks, out_ref = refs[:n_f], refs[-1]
    rows = blocks[0].shape[1]
    for k in range(n_f):
        place = pl.ds(pl.multiple_of((where_ref[0] ^ k) * rows, rows), rows)
        value = blocks[k][...]
        if has_wave:
            value = (refs[n_f][:, place, :] + value.astype(F32)).astype(BF16)
        out_ref[:, place, :] = value


def terms_kernel(chunks, sign, places_ref, whole_ref, v_ref, *refs):
    out_ref = refs[-1]
    lanes = lane_index(v_ref.shape[1:])
    place = (lanes % 64) // (64 // chunks)

    def frequency(b):
        value = v_ref[b].astype(F32)
        turned = pltpu.roll(value, 64, 1)
        turned = jnp.where((lanes < 64) == (sign > 0), -turned, turned)
        weights = [jnp.where(place == a, x, 0.0) for a in range(chunks) for x in (value, turned)]
        weights = jnp.concatenate(weights, axis=0).astype(BF16)
        left = []
        for pos in range(out_ref.shape[0]):
            at = places_ref[pos]
            left.append(jnp.concatenate([whole_ref[p, a, b, at] for a in range(chunks) for p in range(2)], axis=1))
        total = jnp.dot(jnp.concatenate(left, axis=0), weights, preferred_element_type=F32).astype(BF16)
        rows = out_ref.shape[2]
        for pos in range(out_ref.shape[0]):
            out_ref[pos, b] = total[pos * rows : (pos + 1) * rows]

    @pl.loop(0, v_ref.shape[0] // UNROLL)
    def _(i):
        for j in range(UNROLL):
            frequency(i * UNROLL + j)


def add_kernel(n_in, *refs):
    out_ref = refs[-1]
    half = out_ref.shape[0]
    total = refs[0][half : 2 * half].astype(F32)
    for ref in refs[1:n_in]:
        total = total + ref[half : 2 * half].astype(F32)
    out_ref[...] = total.astype(BF16)


def split_kernel(n_in, n_f, where_ref, *refs):
    outs = refs[-n_f:]
    rows = outs[0].shape[1]
    for k in range(n_f):
        place = pl.ds(pl.multiple_of((where_ref[0] ^ k) * rows, rows), rows)
        total = refs[0][0, :, place, :].astype(F32)
        for ref in refs[1:n_in]:
            total = total + ref[0, :, place, :].astype(F32)
        outs[k][...] = total.astype(BF16)


def window_kernel(chunks, n_f, tile, where_ref, limit_ref, inv_ref, fwd_ref, *refs):
    blocks, outs, (gather, scatter) = refs[:n_f], refs[-n_f - 2 : -2], refs[-2:]
    fp, rows, _ = blocks[0].shape
    depth = n_f * fp
    step = depth + PAD
    for k in range(n_f):
        base = (where_ref[0] ^ k) * fp
        for b in range(fp):
            gather[pl.ds(base + b, rows, stride=step), :] = blocks[k][b].astype(F32)
    lanes = lane_index((depth, 128))
    part, place = lanes // 64, (lanes % 64) // (64 // chunks)
    times = lax.broadcasted_iota(jnp.int32, (KEPT, 128), 0)
    width = 64 // chunks
    for first in range(0, rows, tile):
        columns = []
        for r in range(first, first + tile):
            value = gather[pl.ds(r * step, depth), :]
            spread = []
            for a in range(chunks):
                total = value
                for other in range(chunks):
                    if other != a:
                        total = jnp.where(place == other, pltpu.roll(value, ((other - a) * width) % 128, 1), total)
                spread.append(total)
            stacked = [jnp.where(part == p, x, 0.0) for p in range(2) for x in spread]
            columns.append(jnp.concatenate(stacked, axis=0).astype(BF16))
        signal = jnp.dot(inv_ref[...], jnp.concatenate(columns, axis=1), preferred_element_type=F32)
        kept = []
        for i in range(tile):
            limit = limit_ref[pl.ds(first + i, 1), :]
            kept.append(jnp.where(times < limit, signal[:, i * 128 : (i + 1) * 128], 0.0).astype(BF16))
        back = jnp.dot(fwd_ref[...], jnp.concatenate(kept, axis=1), preferred_element_type=F32)
        for i in range(tile):
            total = None
            for p in range(2):
                for a in range(chunks):
                    at = (p * chunks + a) * depth
                    piece = back[at : at + depth, i * 128 : (i + 1) * 128]
                    total = piece if total is None else jnp.where((part == p) & (place == a), piece, total)
            scatter[pl.ds((first + i) * step, depth), :] = total
    for k in range(n_f):
        base = (where_ref[0] ^ k) * fp
        for b in range(fp):
            outs[k][b] = scatter[pl.ds(base + b, rows, stride=step), :].astype(BF16)


def vmem():
    return pl.BlockSpec(memory_space=pltpu.VMEM)


def anywhere():
    return pl.BlockSpec(memory_space=pl.ANY)


def smem():
    return pl.BlockSpec(memory_space=pltpu.SMEM)


def params(mib):
    return pltpu.CompilerParams(vmem_limit_bytes=mib * MIB)


def cost(flops, nbytes):
    return pl.CostEstimate(flops=int(flops), bytes_accessed=int(nbytes), transcendentals=0)


def bf16(*shape):
    return jax.ShapeDtypeStruct(shape, BF16)


class Plan:
    def __init__(self, reflection, direct_wave):
        self.n_f, self.n_s = lax.axis_size("freq"), lax.axis_size("src")
        self.q, self.f_dev, _ = direct_wave.shape
        self.chunks = CHUNKS
        self.fp = self.f_dev // self.chunks
        self.own_rows = self.q // self.n_f
        self.n_chip = self.n_s // 2
        self.bits = self.n_chip.bit_length() - 1
        z, s = lax.axis_index("freq"), lax.axis_index("src")
        chip, self.core = s // 2, s % 2
        self.where = z.reshape(1).astype(jnp.int32)
        orders = np.zeros((2, self.n_chip), np.int32)
        for core in range(2):
            for pos in range(self.n_chip):
                for stage in range(self.bits):
                    if pos >> (self.bits - 1 - stage) & 1:
                        orders[core, pos] ^= self.mask(stage, core)
        orders = jnp.asarray(orders)
        self.near = ((chip ^ orders[self.core]) * 2 + self.core).astype(jnp.int32)
        self.far = ((chip ^ orders[1 - self.core]) * 2 + 1 - self.core).astype(jnp.int32)
        inverse, forward = window_tables(self.n_f * self.f_dev, self.chunks, self.n_f)
        self.tables = [jnp.asarray(inverse), jnp.asarray(forward)]
        self.reflection = reflection.reshape(2, self.chunks, self.fp, self.n_s, self.q, self.q)

    def mask(self, stage, core):
        return 1 << ((stage + core) % self.bits)

    def to_core(self, value):
        return lax.ppermute(value, "src", [(s, s ^ 1) for s in range(self.n_s)])

    def to_chip(self, value, stage):
        pairs = [(s, s ^ (self.mask(stage, s % 2) << 1)) for s in range(self.n_s)]
        return lax.ppermute(value, "src", pairs)

    def to_group(self, value, k):
        return lax.ppermute(value, "freq", [(z, z ^ k) for z in range(self.n_f)])

    def exchange(self, blocks):
        moved = {k: self.to_group(blocks[k], k) for k in range(self.n_f - 1, 0, -1)}
        return [blocks[0]] + [moved[k] for k in range(1, self.n_f)]

    def pack(self, direct_wave):
        return pl.pallas_call(
            functools.partial(pack_kernel, self.chunks, self.f_dev, self.q),
            out_shape=[bf16(self.fp, self.q, 128)] * self.chunks,
            in_specs=[vmem()],
            out_specs=[vmem()] * self.chunks,
            compiler_params=params(OTHER_MIB),
            cost_estimate=cost(WEIGHT, BYTES),
            name="pack",
        )(direct_wave.reshape(self.q * self.f_dev, 128))

    def make_limits(self, first_arrival, after):
        self.limits = pl.pallas_call(
            functools.partial(limits_kernel, self.chunks),
            out_shape=[jax.ShapeDtypeStruct((self.own_rows, 128), jnp.int32)] * self.chunks,
            in_specs=[vmem()] + [anywhere()] * len(after),
            out_specs=[vmem()] * self.chunks,
            compiler_params=params(OTHER_MIB),
            cost_estimate=cost(WEIGHT, BYTES),
            name="limits",
        )(first_arrival, *after)
        return self.limits[:1]

    def waves(self, direct_wave, after):
        n = self.chunks
        return pl.pallas_call(
            functools.partial(wave_kernel, n, self.f_dev, self.q),
            out_shape=[jax.ShapeDtypeStruct((self.fp, self.q, 128), F32)] * n,
            in_specs=[vmem()] + [anywhere()] * len(after),
            out_specs=[vmem()] * n,
            compiler_params=params(OTHER_MIB),
            name="wave",
        )(direct_wave.reshape(self.q * self.f_dev, 128), *after)

    def unpack(self, values, wave=None):
        waves = [] if wave is None else [wave.reshape(self.q * self.f_dev, 128)]
        out = pl.pallas_call(
            functools.partial(unpack_kernel, self.chunks, self.f_dev, self.q, wave is not None),
            out_shape=jax.ShapeDtypeStruct((self.q * self.f_dev, 128), F32),
            in_specs=[vmem()] * (self.chunks + len(waves)),
            out_specs=vmem(),
            compiler_params=params(OTHER_MIB),
            name="unpack",
        )(*values, *waves)
        return out.reshape(self.q, self.f_dev, 128)

    def assemble(self, blocks, wave, after):
        waves = [] if wave is None else [wave]
        return pl.pallas_call(
            functools.partial(assemble_kernel, self.n_f, wave is not None),
            out_shape=bf16(self.fp, self.q, 128),
            in_specs=[smem()] + [vmem()] * (self.n_f + len(waves)) + [anywhere()] * len(after),
            out_specs=vmem(),
            compiler_params=params(OTHER_MIB),
            cost_estimate=cost(WEIGHT, BYTES),
            name="assemble",
        )(self.where, *blocks, *waves, *after)

    def terms(self, vector, places, sign, after):
        return pl.pallas_call(
            functools.partial(terms_kernel, self.chunks, sign),
            out_shape=bf16(self.n_chip, self.fp, self.q, 128),
            in_specs=[smem()] + [vmem()] * 2 + [anywhere()] * len(after),
            out_specs=vmem(),
            compiler_params=params(TERMS_MIB),
            cost_estimate=cost(WEIGHT, BYTES),
            name="terms",
        )(places, self.reflection, vector, *after)

    def add(self, values, half, after):
        return pl.pallas_call(
            functools.partial(add_kernel, len(values)),
            out_shape=bf16(half, self.fp, self.q, 128),
            in_specs=[vmem()] * len(values) + [anywhere()] * len(after),
            out_specs=vmem(),
            compiler_params=params(OTHER_MIB),
            cost_estimate=cost(WEIGHT, BYTES),
            name="add",
        )(*values, *after)

    def split(self, values, after):
        out = bf16(self.fp, self.own_rows, 128)
        return pl.pallas_call(
            functools.partial(split_kernel, len(values), self.n_f),
            out_shape=[out] * self.n_f,
            in_specs=[smem()] + [vmem()] * len(values) + [anywhere()] * len(after),
            out_specs=[vmem()] * self.n_f,
            compiler_params=params(OTHER_MIB),
            cost_estimate=cost(WEIGHT, BYTES),
            name="split",
        )(self.where, *values, *after)

    def window(self, blocks, chunk, after):
        out = bf16(self.fp, self.own_rows, 128)
        depth = self.n_f * self.fp + PAD
        scratch = pltpu.VMEM((self.own_rows * depth, 128), F32)
        return pl.pallas_call(
            functools.partial(window_kernel, self.chunks, self.n_f, min(TILE, self.own_rows)),
            out_shape=[out] * self.n_f,
            in_specs=[smem()] + [vmem()] * (3 + self.n_f) + [anywhere()] * len(after),
            out_specs=[vmem()] * self.n_f,
            scratch_shapes=[scratch, scratch],
            compiler_params=params(OTHER_MIB),
            cost_estimate=cost(WEIGHT, BYTES),
            name="window",
        )(self.where, self.limits[chunk], *self.tables, *blocks, *after)


class Chain:
    def __init__(self, plan, chunk, vector):
        self.plan, self.chunk, self.wave = plan, chunk, None
        self.vector, self.done, self.minus = vector, 0, None
        self.todo = self.theta()

    def theta(self):
        return [self.far, self.near] + [self.add] * self.plan.bits + [self.split, self.window, self.assemble]

    def step(self, after):
        return self.todo.pop(0)(after)

    def sign(self):
        return 1 if self.done % 2 == 0 else -1

    def far(self, after):
        out = self.plan.terms(self.vector, self.plan.far, self.sign(), after)
        self.arriving = self.plan.to_core(out)
        return [out]

    def near(self, after):
        out = self.plan.terms(self.vector, self.plan.near, self.sign(), after)
        self.addends, self.half = [out, self.arriving], self.plan.n_chip
        return [out]

    def add(self, after):
        plan = self.plan
        self.half //= 2
        send = plan.add(self.addends, self.half, after)
        self.addends.append(plan.to_chip(send, len(self.addends) - 2))
        return [send]

    def split(self, after):
        blocks = self.plan.split(self.addends, after)
        self.blocks = self.plan.exchange(blocks)
        return [blocks[0]]

    def window(self, after):
        blocks = self.plan.window(self.blocks, self.chunk, after)
        self.blocks = self.plan.exchange(blocks)
        return [blocks[0]]

    def assemble(self, after):
        self.done += 1
        wave = self.wave if self.done % 2 == 0 and self.done < 2 * ITERS else None
        self.vector = self.plan.assemble(self.blocks, wave, after)
        if self.done == 2 * ITERS - 1:
            self.minus = self.vector
        self.todo = self.theta()
        return [self.vector]


def local(reflection, direct_wave, first_arrival):
    plan = Plan(reflection, direct_wave)
    plus = plan.pack(direct_wave)
    chains = [Chain(plan, i, plus[i]) for i in range(plan.chunks)]
    first, second = chains[0], chains[-1]
    after = []
    for step in range(2 * ITERS):
        for place, chain in enumerate([first, first, second, first, second, second]):
            if step and place in (0, 2):
                after = chain.step(after)
            after = chain.step(after)
        if step == 0:
            after = plan.make_limits(first_arrival, after)
        if step == 1:
            waves = plan.waves(direct_wave, after)
            after = waves[:1]
            for chain, wave in zip(chains, waves):
                chain.wave = wave
        for _ in range(1 + plan.bits):
            for chain in chains:
                after = chain.step(after)
    for chain in chains:
        after = chain.step(after)
    return plan.unpack([c.minus for c in chains]), plan.unpack([c.vector for c in chains], direct_wave)


def solution(mesh):
    in_specs = (P(None, "freq", None, "src"), P("src", "freq", None), P(("src", "freq"), None))
    out_specs = (P("src", "freq", None), P("src", "freq", None))
    return jax.shard_map(local, mesh=mesh, in_specs=in_specs, out_specs=out_specs, check_vma=False)
```

```python
import functools
import math

import jax
import jax.numpy as jnp
import ml_dtypes
import numpy as np
from jax import lax
from jax.experimental import pallas as pl
from jax.experimental.pallas import tpu as pltpu
from jax.sharding import PartitionSpec as P

NT = 512
ITERS = 2
KEPT = 192
CHUNKS = 2
MIB = 1 << 20
WEIGHT = 3e9
UNROLL = 8
BYTES = MIB
ORDER = "00011011"
START = "000111"
TILE = 16
PAD = 4
TERMS_MIB = 32
OTHER_MIB = 12
BF16, F32 = jnp.bfloat16, jnp.float32


def window_tables(nfreq, chunks, groups):
    freqs = np.arange(1, nfreq + 1)
    times = np.arange(KEPT)
    phase = ((freqs[:, None] * times[None, :]) % NT).astype(np.float32) * np.float32(2.0 * math.pi / NT)
    parts = np.stack([np.cos(phase), -np.sin(phase)])
    inverse = (parts * np.float32(2.0 / NT)).astype(ml_dtypes.bfloat16)
    forward = parts.astype(ml_dtypes.bfloat16).astype(np.float32) * np.where(times == 0, 1.0, 2.0)
    forward = forward.astype(ml_dtypes.bfloat16)

    def rows(table):
        table = table.reshape(2, groups, chunks, nfreq // groups // chunks, KEPT)
        return table.transpose(0, 2, 1, 3, 4).reshape(2 * nfreq, KEPT)

    return np.ascontiguousarray(rows(inverse).T), rows(forward)


def lane_index(shape):
    return lax.broadcasted_iota(jnp.int32, shape, len(shape) - 1)


def to_chunks(by_sub, lanes):
    n = len(by_sub)
    if n == 1:
        return by_sub
    width = 64 // n
    place = (lanes % 64) // width
    result = []
    for other in range(n):
        total = None
        for a in range(n):
            shift = ((a - other) * width) % 128
            moved = pltpu.roll(by_sub[a], shift, 1) if shift else by_sub[a]
            total = moved if total is None else jnp.where(place == a, moved, total)
        result.append(total)
    return result


def pack_kernel(chunks, f_dev, rows, dw_ref, *out_refs):
    fp = f_dev // chunks
    lanes = lane_index((rows, 128))

    @pl.loop(0, fp)
    def _(b):
        values = [dw_ref[pl.ds(a * fp + b, rows, stride=f_dev), :] for a in range(chunks)]
        for out_ref, value in zip(out_refs, to_chunks(values, lanes)):
            out_ref[b] = value.astype(BF16)


def limits_kernel(chunks, arrival_ref, *refs):
    width = 64 // chunks
    for chunk, out_ref in enumerate(refs[-chunks:]):
        limit = arrival_ref[:, chunk * width : (chunk + 1) * width]
        out_ref[...] = jnp.concatenate([limit] * (2 * chunks), axis=1)


def wave_kernel(chunks, f_dev, rows, dw_ref, *refs):
    fp = f_dev // chunks
    lanes = lane_index((rows, 128))

    @pl.loop(0, fp)
    def _(b):
        values = [dw_ref[pl.ds(a * fp + b, rows, stride=f_dev), :] for a in range(chunks)]
        for out_ref, value in zip(refs[-chunks:], to_chunks(values, lanes)):
            out_ref[b] = value


def unpack_kernel(chunks, f_dev, rows, has_wave, *refs):
    fp = f_dev // chunks
    lanes = lane_index((rows, 128))
    v_refs, out_ref = refs[:chunks], refs[-1]
    for b in range(fp):
        values = [v_refs[chunk][b].astype(F32) for chunk in range(chunks)]
        for a, value in enumerate(to_chunks(values, lanes)):
            place = pl.ds(a * fp + b, rows, stride=f_dev)
            if has_wave:
                value = value + refs[chunks][place, :]
            out_ref[place, :] = value


def assemble_kernel(n_f, has_wave, where_ref, *refs):
    blocks, out_ref = refs[:n_f], refs[-1]
    rows = blocks[0].shape[1]
    for k in range(n_f):
        place = pl.ds(pl.multiple_of((where_ref[0] ^ k) * rows, rows), rows)
        value = blocks[k][...]
        if has_wave:
            value = (refs[n_f][:, place, :] + value.astype(F32)).astype(BF16)
        out_ref[:, place, :] = value


def terms_kernel(chunks, sign, places_ref, whole_ref, v_ref, *refs):
    out_ref = refs[-1]
    lanes = lane_index(v_ref.shape[1:])
    place = (lanes % 64) // (64 // chunks)

    def frequency(b):
        value = v_ref[b].astype(F32)
        turned = pltpu.roll(value, 64, 1)
        turned = jnp.where((lanes < 64) == (sign > 0), -turned, turned)
        weights = [jnp.where(place == a, x, 0.0) for a in range(chunks) for x in (value, turned)]
        weights = jnp.concatenate(weights, axis=0).astype(BF16)
        left = []
        for pos in range(out_ref.shape[0]):
            at = places_ref[pos]
            left.append(jnp.concatenate([whole_ref[p, a, b, at] for a in range(chunks) for p in range(2)], axis=1))
        total = jnp.dot(jnp.concatenate(left, axis=0), weights, preferred_element_type=F32).astype(BF16)
        rows = out_ref.shape[2]
        for pos in range(out_ref.shape[0]):
            out_ref[pos, b] = total[pos * rows : (pos + 1) * rows]

    @pl.loop(0, v_ref.shape[0] // UNROLL)
    def _(i):
        for j in range(UNROLL):
            frequency(i * UNROLL + j)


def add_kernel(n_in, *refs):
    out_ref = refs[-1]
    half = out_ref.shape[0]
    total = refs[0][half : 2 * half].astype(F32)
    for ref in refs[1:n_in]:
        total = total + ref[half : 2 * half].astype(F32)
    out_ref[...] = total.astype(BF16)


def split_kernel(n_in, n_f, where_ref, *refs):
    outs = refs[-n_f:]
    rows = outs[0].shape[1]
    for k in range(n_f):
        place = pl.ds(pl.multiple_of((where_ref[0] ^ k) * rows, rows), rows)
        total = refs[0][0, :, place, :].astype(F32)
        for ref in refs[1:n_in]:
            total = total + ref[0, :, place, :].astype(F32)
        outs[k][...] = total.astype(BF16)


def window_kernel(chunks, n_f, tile, where_ref, limit_ref, inv_ref, fwd_ref, *refs):
    blocks, outs, (gather, scatter) = refs[:n_f], refs[-n_f - 2 : -2], refs[-2:]
    fp, rows, _ = blocks[0].shape
    depth = n_f * fp
    step = depth + PAD
    for k in range(n_f):
        base = (where_ref[0] ^ k) * fp
        for b in range(fp):
            gather[pl.ds(base + b, rows, stride=step), :] = blocks[k][b].astype(F32)
    lanes = lane_index((depth, 128))
    part, place = lanes // 64, (lanes % 64) // (64 // chunks)
    times = lax.broadcasted_iota(jnp.int32, (KEPT, 128), 0)
    width = 64 // chunks
    for first in range(0, rows, tile):
        columns = []
        for r in range(first, first + tile):
            value = gather[pl.ds(r * step, depth), :]
            spread = []
            for a in range(chunks):
                total = value
                for other in range(chunks):
                    if other != a:
                        total = jnp.where(place == other, pltpu.roll(value, ((other - a) * width) % 128, 1), total)
                spread.append(total)
            stacked = [jnp.where(part == p, x, 0.0) for p in range(2) for x in spread]
            columns.append(jnp.concatenate(stacked, axis=0).astype(BF16))
        signal = jnp.dot(inv_ref[...], jnp.concatenate(columns, axis=1), preferred_element_type=F32)
        kept = []
        for i in range(tile):
            limit = limit_ref[pl.ds(first + i, 1), :]
            kept.append(jnp.where(times < limit, signal[:, i * 128 : (i + 1) * 128], 0.0).astype(BF16))
        back = jnp.dot(fwd_ref[...], jnp.concatenate(kept, axis=1), preferred_element_type=F32)
        for i in range(tile):
            total = None
            for p in range(2):
                for a in range(chunks):
                    at = (p * chunks + a) * depth
                    piece = back[at : at + depth, i * 128 : (i + 1) * 128]
                    total = piece if total is None else jnp.where((part == p) & (place == a), piece, total)
            scatter[pl.ds((first + i) * step, depth), :] = total
    for k in range(n_f):
        base = (where_ref[0] ^ k) * fp
        for b in range(fp):
            outs[k][b] = scatter[pl.ds(base + b, rows, stride=step), :].astype(BF16)


def vmem():
    return pl.BlockSpec(memory_space=pltpu.VMEM)


def anywhere():
    return pl.BlockSpec(memory_space=pl.ANY)


def smem():
    return pl.BlockSpec(memory_space=pltpu.SMEM)


def params(mib):
    return pltpu.CompilerParams(vmem_limit_bytes=mib * MIB)


def cost(flops, nbytes):
    return pl.CostEstimate(flops=int(flops), bytes_accessed=int(nbytes), transcendentals=0)


def bf16(*shape):
    return jax.ShapeDtypeStruct(shape, BF16)


class Plan:
    def __init__(self, reflection, direct_wave):
        self.n_f, self.n_s = lax.axis_size("freq"), lax.axis_size("src")
        self.q, self.f_dev, _ = direct_wave.shape
        self.chunks = CHUNKS
        self.fp = self.f_dev // self.chunks
        self.own_rows = self.q // self.n_f
        self.n_chip = self.n_s // 2
        self.bits = self.n_chip.bit_length() - 1
        z, s = lax.axis_index("freq"), lax.axis_index("src")
        chip, self.core = s // 2, s % 2
        self.where = z.reshape(1).astype(jnp.int32)
        orders = np.zeros((2, self.n_chip), np.int32)
        for core in range(2):
            for pos in range(self.n_chip):
                for stage in range(self.bits):
                    if pos >> (self.bits - 1 - stage) & 1:
                        orders[core, pos] ^= self.mask(stage, core)
        orders = jnp.asarray(orders)
        self.near = ((chip ^ orders[self.core]) * 2 + self.core).astype(jnp.int32)
        self.far = ((chip ^ orders[1 - self.core]) * 2 + 1 - self.core).astype(jnp.int32)
        inverse, forward = window_tables(self.n_f * self.f_dev, self.chunks, self.n_f)
        self.tables = [jnp.asarray(inverse), jnp.asarray(forward)]
        self.reflection = reflection.reshape(2, self.chunks, self.fp, self.n_s, self.q, self.q)

    def mask(self, stage, core):
        return 1 << ((stage + core) % self.bits)

    def to_core(self, value):
        return lax.ppermute(value, "src", [(s, s ^ 1) for s in range(self.n_s)])

    def to_chip(self, value, stage):
        pairs = [(s, s ^ (self.mask(stage, s % 2) << 1)) for s in range(self.n_s)]
        return lax.ppermute(value, "src", pairs)

    def to_group(self, value, k):
        return lax.ppermute(value, "freq", [(z, z ^ k) for z in range(self.n_f)])

    def exchange(self, blocks):
        moved = {k: self.to_group(blocks[k], k) for k in range(self.n_f - 1, 0, -1)}
        return [blocks[0]] + [moved[k] for k in range(1, self.n_f)]

    def pack(self, direct_wave):
        return pl.pallas_call(
            functools.partial(pack_kernel, self.chunks, self.f_dev, self.q),
            out_shape=[bf16(self.fp, self.q, 128)] * self.chunks,
            in_specs=[vmem()],
            out_specs=[vmem()] * self.chunks,
            compiler_params=params(OTHER_MIB),
            cost_estimate=cost(WEIGHT, BYTES),
            name="pack",
        )(direct_wave.reshape(self.q * self.f_dev, 128))

    def make_limits(self, first_arrival, after):
        self.limits = pl.pallas_call(
            functools.partial(limits_kernel, self.chunks),
            out_shape=[jax.ShapeDtypeStruct((self.own_rows, 128), jnp.int32)] * self.chunks,
            in_specs=[vmem()] + [anywhere()] * len(after),
            out_specs=[vmem()] * self.chunks,
            compiler_params=params(OTHER_MIB),
            cost_estimate=cost(WEIGHT, BYTES),
            name="limits",
        )(first_arrival, *after)
        return self.limits[:1]

    def waves(self, direct_wave, after):
        n = self.chunks
        return pl.pallas_call(
            functools.partial(wave_kernel, n, self.f_dev, self.q),
            out_shape=[jax.ShapeDtypeStruct((self.fp, self.q, 128), F32)] * n,
            in_specs=[vmem()] + [anywhere()] * len(after),
            out_specs=[vmem()] * n,
            compiler_params=params(OTHER_MIB),
            name="wave",
        )(direct_wave.reshape(self.q * self.f_dev, 128), *after)

    def unpack(self, values, wave=None):
        waves = [] if wave is None else [wave.reshape(self.q * self.f_dev, 128)]
        out = pl.pallas_call(
            functools.partial(unpack_kernel, self.chunks, self.f_dev, self.q, wave is not None),
            out_shape=jax.ShapeDtypeStruct((self.q * self.f_dev, 128), F32),
            in_specs=[vmem()] * (self.chunks + len(waves)),
            out_specs=vmem(),
            compiler_params=params(OTHER_MIB),
            name="unpack",
        )(*values, *waves)
        return out.reshape(self.q, self.f_dev, 128)

    def assemble(self, blocks, wave, after):
        waves = [] if wave is None else [wave]
        return pl.pallas_call(
            functools.partial(assemble_kernel, self.n_f, wave is not None),
            out_shape=bf16(self.fp, self.q, 128),
            in_specs=[smem()] + [vmem()] * (self.n_f + len(waves)) + [anywhere()] * len(after),
            out_specs=vmem(),
            compiler_params=params(OTHER_MIB),
            cost_estimate=cost(WEIGHT, BYTES),
            name="assemble",
        )(self.where, *blocks, *waves, *after)

    def terms(self, vector, places, sign, after):
        return pl.pallas_call(
            functools.partial(terms_kernel, self.chunks, sign),
            out_shape=bf16(self.n_chip, self.fp, self.q, 128),
            in_specs=[smem()] + [vmem()] * 2 + [anywhere()] * len(after),
            out_specs=vmem(),
            compiler_params=params(TERMS_MIB),
            cost_estimate=cost(WEIGHT, BYTES),
            name="terms",
        )(places, self.reflection, vector, *after)

    def add(self, values, half, after):
        return pl.pallas_call(
            functools.partial(add_kernel, len(values)),
            out_shape=bf16(half, self.fp, self.q, 128),
            in_specs=[vmem()] * len(values) + [anywhere()] * len(after),
            out_specs=vmem(),
            compiler_params=params(OTHER_MIB),
            cost_estimate=cost(WEIGHT, BYTES),
            name="add",
        )(*values, *after)

    def split(self, values, after):
        out = bf16(self.fp, self.own_rows, 128)
        return pl.pallas_call(
            functools.partial(split_kernel, len(values), self.n_f),
            out_shape=[out] * self.n_f,
            in_specs=[smem()] + [vmem()] * len(values) + [anywhere()] * len(after),
            out_specs=[vmem()] * self.n_f,
            compiler_params=params(OTHER_MIB),
            cost_estimate=cost(WEIGHT, BYTES),
            name="split",
        )(self.where, *values, *after)

    def window(self, blocks, chunk, after):
        out = bf16(self.fp, self.own_rows, 128)
        depth = self.n_f * self.fp + PAD
        scratch = pltpu.VMEM((self.own_rows * depth, 128), F32)
        return pl.pallas_call(
            functools.partial(window_kernel, self.chunks, self.n_f, min(TILE, self.own_rows)),
            out_shape=[out] * self.n_f,
            in_specs=[smem()] + [vmem()] * (3 + self.n_f) + [anywhere()] * len(after),
            out_specs=[vmem()] * self.n_f,
            scratch_shapes=[scratch, scratch],
            compiler_params=params(OTHER_MIB),
            cost_estimate=cost(WEIGHT, BYTES),
            name="window",
        )(self.where, self.limits[chunk], *self.tables, *blocks, *after)


class Chain:
    def __init__(self, plan, chunk, vector):
        self.plan, self.chunk, self.wave = plan, chunk, None
        self.vector, self.done, self.minus = vector, 0, None
        self.todo = self.theta()

    def theta(self):
        return [self.far, self.near] + [self.add] * self.plan.bits + [self.split, self.window, self.assemble]

    def step(self, after):
        return self.todo.pop(0)(after)

    def sign(self):
        return 1 if self.done % 2 == 0 else -1

    def far(self, after):
        out = self.plan.terms(self.vector, self.plan.far, self.sign(), after)
        self.arriving = self.plan.to_core(out)
        return [out]

    def near(self, after):
        out = self.plan.terms(self.vector, self.plan.near, self.sign(), after)
        self.addends, self.half = [out, self.arriving], self.plan.n_chip
        return [out]

    def add(self, after):
        plan = self.plan
        self.half //= 2
        send = plan.add(self.addends, self.half, after)
        self.addends.append(plan.to_chip(send, len(self.addends) - 2))
        return [send]

    def split(self, after):
        blocks = self.plan.split(self.addends, after)
        self.blocks = self.plan.exchange(blocks)
        return [blocks[0]]

    def window(self, after):
        blocks = self.plan.window(self.blocks, self.chunk, after)
        self.blocks = self.plan.exchange(blocks)
        return [blocks[0]]

    def assemble(self, after):
        self.done += 1
        wave = self.wave if self.done % 2 == 0 and self.done < 2 * ITERS else None
        self.vector = self.plan.assemble(self.blocks, wave, after)
        if self.done == 2 * ITERS - 1:
            self.minus = self.vector
        self.todo = self.theta()
        return [self.vector]


def local(reflection, direct_wave, first_arrival):
    plan = Plan(reflection, direct_wave)
    plus = plan.pack(direct_wave)
    chains = [Chain(plan, i, plus[i]) for i in range(plan.chunks)]
    after = []
    for step in range(2 * ITERS):
        for i in ORDER if step else START:
            after = chains[int(i)].step(after)
        if step == 0:
            after = plan.make_limits(first_arrival, after)
        if step == 1:
            waves = plan.waves(direct_wave, after)
            after = waves[:1]
            for chain, wave in zip(chains, waves):
                chain.wave = wave
        for _ in range(1 + plan.bits):
            for chain in chains:
                after = chain.step(after)
    for chain in chains:
        after = chain.step(after)
    return plan.unpack([c.minus for c in chains]), plan.unpack([c.vector for c in chains], direct_wave)


def solution(mesh):
    in_specs = (P(None, "freq", None, "src"), P("src", "freq", None), P(("src", "freq"), None))
    out_specs = (P("src", "freq", None), P("src", "freq", None))
    return jax.shard_map(local, mesh=mesh, in_specs=in_specs, out_specs=out_specs, check_vma=False)
```

```python
import functools
import math

import jax
import jax.numpy as jnp
import ml_dtypes
import numpy as np
from jax import lax
from jax.experimental import pallas as pl
from jax.experimental.pallas import tpu as pltpu
from jax.sharding import PartitionSpec as P

NT = 512
ITERS = 2
KEPT = 192
CHUNKS = 2
MIB = 1 << 20
WEIGHT = 3e9
UNROLL = 8
BYTES = MIB
ORDER = "00011011"
START = "000111"
TILE = 16
PAD = 4
TERMS_MIB = 32
OTHER_MIB = 12
BF16, F32 = jnp.bfloat16, jnp.float32


def window_tables(nfreq, chunks, groups):
    freqs = np.arange(1, nfreq + 1)
    times = np.arange(KEPT)
    phase = ((freqs[:, None] * times[None, :]) % NT).astype(np.float32) * np.float32(2.0 * math.pi / NT)
    parts = np.stack([np.cos(phase), -np.sin(phase)])
    inverse = (parts * np.float32(2.0 / NT)).astype(ml_dtypes.bfloat16)
    forward = parts.astype(ml_dtypes.bfloat16).astype(np.float32) * np.where(times == 0, 1.0, 2.0)
    forward = forward.astype(ml_dtypes.bfloat16)

    def rows(table):
        table = table.reshape(2, groups, chunks, nfreq // groups // chunks, KEPT)
        return table.transpose(0, 2, 1, 3, 4).reshape(2 * nfreq, KEPT)

    return np.ascontiguousarray(rows(inverse).T), rows(forward)


def lane_index(shape):
    return lax.broadcasted_iota(jnp.int32, shape, len(shape) - 1)


def to_chunks(by_sub, lanes):
    n = len(by_sub)
    if n == 1:
        return by_sub
    width = 64 // n
    place = (lanes % 64) // width
    result = []
    for other in range(n):
        total = None
        for a in range(n):
            shift = ((a - other) * width) % 128
            moved = pltpu.roll(by_sub[a], shift, 1) if shift else by_sub[a]
            total = moved if total is None else jnp.where(place == a, moved, total)
        result.append(total)
    return result


def pack_kernel(chunks, f_dev, rows, dw_ref, *out_refs):
    fp = f_dev // chunks
    lanes = lane_index((rows, 128))

    @pl.loop(0, fp)
    def _(b):
        values = [dw_ref[pl.ds(a * fp + b, rows, stride=f_dev), :] for a in range(chunks)]
        for out_ref, value in zip(out_refs, to_chunks(values, lanes)):
            out_ref[b] = value.astype(BF16)


def limits_kernel(chunks, arrival_ref, *refs):
    width = 64 // chunks
    for chunk, out_ref in enumerate(refs[-chunks:]):
        limit = arrival_ref[:, chunk * width : (chunk + 1) * width]
        out_ref[...] = jnp.concatenate([limit] * (2 * chunks), axis=1)


def wave_kernel(chunks, f_dev, rows, dw_ref, *refs):
    fp = f_dev // chunks
    lanes = lane_index((rows, 128))

    @pl.loop(0, fp)
    def _(b):
        values = [dw_ref[pl.ds(a * fp + b, rows, stride=f_dev), :] for a in range(chunks)]
        for out_ref, value in zip(refs[-chunks:], to_chunks(values, lanes)):
            out_ref[b] = value


def unpack_kernel(chunks, f_dev, rows, has_wave, *refs):
    fp = f_dev // chunks
    lanes = lane_index((rows, 128))
    v_refs, out_ref = refs[:chunks], refs[-1]
    for b in range(fp):
        values = [v_refs[chunk][b].astype(F32) for chunk in range(chunks)]
        for a, value in enumerate(to_chunks(values, lanes)):
            place = pl.ds(a * fp + b, rows, stride=f_dev)
            if has_wave:
                value = value + refs[chunks][place, :]
            out_ref[place, :] = value


def assemble_kernel(n_f, has_wave, where_ref, *refs):
    blocks, out_ref = refs[:n_f], refs[-1]
    rows = blocks[0].shape[1]
    for k in range(n_f):
        place = pl.ds(pl.multiple_of((where_ref[0] ^ k) * rows, rows), rows)
        value = blocks[k][...]
        if has_wave:
            value = (refs[n_f][:, place, :] + value.astype(F32)).astype(BF16)
        out_ref[:, place, :] = value


def terms_kernel(chunks, sign, places_ref, whole_ref, v_ref, *refs):
    out_ref = refs[-1]
    lanes = lane_index(v_ref.shape[1:])
    place = (lanes % 64) // (64 // chunks)
    signs = jnp.where((lanes < 64) == (sign > 0), -1.0, 1.0).astype(BF16)
    masks = [jnp.where(place == a, 1.0, 0.0).astype(BF16) for a in range(chunks)]
    masks = [(mask, mask * signs) for mask in masks]

    def frequency(b):
        value = v_ref[b]
        turned = pltpu.roll(value.astype(F32), 64, 1).astype(BF16)
        weights = jnp.concatenate([x * m for pair in masks for x, m in zip((value, turned), pair)], axis=0)
        left = []
        for pos in range(out_ref.shape[0]):
            at = places_ref[pos]
            left.append(jnp.concatenate([whole_ref[p, a, b, at] for a in range(chunks) for p in range(2)], axis=1))
        total = jnp.dot(jnp.concatenate(left, axis=0), weights, preferred_element_type=F32).astype(BF16)
        rows = out_ref.shape[2]
        for pos in range(out_ref.shape[0]):
            out_ref[pos, b] = total[pos * rows : (pos + 1) * rows]

    @pl.loop(0, v_ref.shape[0] // UNROLL)
    def _(i):
        for j in range(UNROLL):
            frequency(i * UNROLL + j)


def add_kernel(n_in, *refs):
    out_ref = refs[-1]
    half = out_ref.shape[0]
    total = refs[0][half : 2 * half].astype(F32)
    for ref in refs[1:n_in]:
        total = total + ref[half : 2 * half].astype(F32)
    out_ref[...] = total.astype(BF16)


def split_kernel(n_in, n_f, where_ref, *refs):
    outs = refs[-n_f:]
    rows = outs[0].shape[1]
    for k in range(n_f):
        place = pl.ds(pl.multiple_of((where_ref[0] ^ k) * rows, rows), rows)
        total = refs[0][0, :, place, :].astype(F32)
        for ref in refs[1:n_in]:
            total = total + ref[0, :, place, :].astype(F32)
        outs[k][...] = total.astype(BF16)


def window_kernel(chunks, n_f, tile, where_ref, limit_ref, inv_ref, fwd_ref, *refs):
    blocks, outs, (gather, scatter) = refs[:n_f], refs[-n_f - 2 : -2], refs[-2:]
    fp, rows, _ = blocks[0].shape
    depth = n_f * fp
    step = depth + PAD
    for k in range(n_f):
        base = (where_ref[0] ^ k) * fp
        for b in range(fp):
            gather[pl.ds(base + b, rows, stride=step), :] = blocks[k][b].astype(F32)
    lanes = lane_index((depth, 128))
    part, place = lanes // 64, (lanes % 64) // (64 // chunks)
    times = lax.broadcasted_iota(jnp.int32, (KEPT, 128), 0)
    width = 64 // chunks
    for first in range(0, rows, tile):
        columns = []
        for r in range(first, first + tile):
            value = gather[pl.ds(r * step, depth), :]
            spread = []
            for a in range(chunks):
                total = value
                for other in range(chunks):
                    if other != a:
                        total = jnp.where(place == other, pltpu.roll(value, ((other - a) * width) % 128, 1), total)
                spread.append(total)
            stacked = [jnp.where(part == p, x, 0.0) for p in range(2) for x in spread]
            columns.append(jnp.concatenate(stacked, axis=0).astype(BF16))
        signal = jnp.dot(inv_ref[...], jnp.concatenate(columns, axis=1), preferred_element_type=F32)
        kept = []
        for i in range(tile):
            limit = limit_ref[pl.ds(first + i, 1), :]
            kept.append(jnp.where(times < limit, signal[:, i * 128 : (i + 1) * 128], 0.0).astype(BF16))
        back = jnp.dot(fwd_ref[...], jnp.concatenate(kept, axis=1), preferred_element_type=F32)
        for i in range(tile):
            total = None
            for p in range(2):
                for a in range(chunks):
                    at = (p * chunks + a) * depth
                    piece = back[at : at + depth, i * 128 : (i + 1) * 128]
                    total = piece if total is None else jnp.where((part == p) & (place == a), piece, total)
            scatter[pl.ds((first + i) * step, depth), :] = total
    for k in range(n_f):
        base = (where_ref[0] ^ k) * fp
        for b in range(fp):
            outs[k][b] = scatter[pl.ds(base + b, rows, stride=step), :].astype(BF16)


def vmem():
    return pl.BlockSpec(memory_space=pltpu.VMEM)


def anywhere():
    return pl.BlockSpec(memory_space=pl.ANY)


def smem():
    return pl.BlockSpec(memory_space=pltpu.SMEM)


def params(mib):
    return pltpu.CompilerParams(vmem_limit_bytes=mib * MIB)


def cost(flops, nbytes):
    return pl.CostEstimate(flops=int(flops), bytes_accessed=int(nbytes), transcendentals=0)


def bf16(*shape):
    return jax.ShapeDtypeStruct(shape, BF16)


class Plan:
    def __init__(self, reflection, direct_wave):
        self.n_f, self.n_s = lax.axis_size("freq"), lax.axis_size("src")
        self.q, self.f_dev, _ = direct_wave.shape
        self.chunks = CHUNKS
        self.fp = self.f_dev // self.chunks
        self.own_rows = self.q // self.n_f
        self.n_chip = self.n_s // 2
        self.bits = self.n_chip.bit_length() - 1
        z, s = lax.axis_index("freq"), lax.axis_index("src")
        chip, self.core = s // 2, s % 2
        self.where = z.reshape(1).astype(jnp.int32)
        orders = np.zeros((2, self.n_chip), np.int32)
        for core in range(2):
            for pos in range(self.n_chip):
                for stage in range(self.bits):
                    if pos >> (self.bits - 1 - stage) & 1:
                        orders[core, pos] ^= self.mask(stage, core)
        orders = jnp.asarray(orders)
        self.near = ((chip ^ orders[self.core]) * 2 + self.core).astype(jnp.int32)
        self.far = ((chip ^ orders[1 - self.core]) * 2 + 1 - self.core).astype(jnp.int32)
        inverse, forward = window_tables(self.n_f * self.f_dev, self.chunks, self.n_f)
        self.tables = [jnp.asarray(inverse), jnp.asarray(forward)]
        self.reflection = reflection.reshape(2, self.chunks, self.fp, self.n_s, self.q, self.q)

    def mask(self, stage, core):
        return 1 << ((stage + core) % self.bits)

    def to_core(self, value):
        return lax.ppermute(value, "src", [(s, s ^ 1) for s in range(self.n_s)])

    def to_chip(self, value, stage):
        pairs = [(s, s ^ (self.mask(stage, s % 2) << 1)) for s in range(self.n_s)]
        return lax.ppermute(value, "src", pairs)

    def to_group(self, value, k):
        return lax.ppermute(value, "freq", [(z, z ^ k) for z in range(self.n_f)])

    def exchange(self, blocks):
        moved = {k: self.to_group(blocks[k], k) for k in range(self.n_f - 1, 0, -1)}
        return [blocks[0]] + [moved[k] for k in range(1, self.n_f)]

    def pack(self, direct_wave):
        return pl.pallas_call(
            functools.partial(pack_kernel, self.chunks, self.f_dev, self.q),
            out_shape=[bf16(self.fp, self.q, 128)] * self.chunks,
            in_specs=[vmem()],
            out_specs=[vmem()] * self.chunks,
            compiler_params=params(OTHER_MIB),
            cost_estimate=cost(WEIGHT, BYTES),
            name="pack",
        )(direct_wave.reshape(self.q * self.f_dev, 128))

    def make_limits(self, first_arrival, after):
        self.limits = pl.pallas_call(
            functools.partial(limits_kernel, self.chunks),
            out_shape=[jax.ShapeDtypeStruct((self.own_rows, 128), jnp.int32)] * self.chunks,
            in_specs=[vmem()] + [anywhere()] * len(after),
            out_specs=[vmem()] * self.chunks,
            compiler_params=params(OTHER_MIB),
            cost_estimate=cost(WEIGHT, BYTES),
            name="limits",
        )(first_arrival, *after)
        return self.limits[:1]

    def waves(self, direct_wave, after):
        n = self.chunks
        return pl.pallas_call(
            functools.partial(wave_kernel, n, self.f_dev, self.q),
            out_shape=[jax.ShapeDtypeStruct((self.fp, self.q, 128), F32)] * n,
            in_specs=[vmem()] + [anywhere()] * len(after),
            out_specs=[vmem()] * n,
            compiler_params=params(OTHER_MIB),
            name="wave",
        )(direct_wave.reshape(self.q * self.f_dev, 128), *after)

    def unpack(self, values, wave=None):
        waves = [] if wave is None else [wave.reshape(self.q * self.f_dev, 128)]
        out = pl.pallas_call(
            functools.partial(unpack_kernel, self.chunks, self.f_dev, self.q, wave is not None),
            out_shape=jax.ShapeDtypeStruct((self.q * self.f_dev, 128), F32),
            in_specs=[vmem()] * (self.chunks + len(waves)),
            out_specs=vmem(),
            compiler_params=params(OTHER_MIB),
            name="unpack",
        )(*values, *waves)
        return out.reshape(self.q, self.f_dev, 128)

    def assemble(self, blocks, wave, after):
        waves = [] if wave is None else [wave]
        return pl.pallas_call(
            functools.partial(assemble_kernel, self.n_f, wave is not None),
            out_shape=bf16(self.fp, self.q, 128),
            in_specs=[smem()] + [vmem()] * (self.n_f + len(waves)) + [anywhere()] * len(after),
            out_specs=vmem(),
            compiler_params=params(OTHER_MIB),
            cost_estimate=cost(WEIGHT, BYTES),
            name="assemble",
        )(self.where, *blocks, *waves, *after)

    def terms(self, vector, places, sign, after):
        return pl.pallas_call(
            functools.partial(terms_kernel, self.chunks, sign),
            out_shape=bf16(self.n_chip, self.fp, self.q, 128),
            in_specs=[smem()] + [vmem()] * 2 + [anywhere()] * len(after),
            out_specs=vmem(),
            compiler_params=params(TERMS_MIB),
            cost_estimate=cost(WEIGHT, BYTES),
            name="terms",
        )(places, self.reflection, vector, *after)

    def add(self, values, half, after):
        return pl.pallas_call(
            functools.partial(add_kernel, len(values)),
            out_shape=bf16(half, self.fp, self.q, 128),
            in_specs=[vmem()] * len(values) + [anywhere()] * len(after),
            out_specs=vmem(),
            compiler_params=params(OTHER_MIB),
            cost_estimate=cost(WEIGHT, BYTES),
            name="add",
        )(*values, *after)

    def split(self, values, after):
        out = bf16(self.fp, self.own_rows, 128)
        return pl.pallas_call(
            functools.partial(split_kernel, len(values), self.n_f),
            out_shape=[out] * self.n_f,
            in_specs=[smem()] + [vmem()] * len(values) + [anywhere()] * len(after),
            out_specs=[vmem()] * self.n_f,
            compiler_params=params(OTHER_MIB),
            cost_estimate=cost(WEIGHT, BYTES),
            name="split",
        )(self.where, *values, *after)

    def window(self, blocks, chunk, after):
        out = bf16(self.fp, self.own_rows, 128)
        depth = self.n_f * self.fp + PAD
        scratch = pltpu.VMEM((self.own_rows * depth, 128), F32)
        return pl.pallas_call(
            functools.partial(window_kernel, self.chunks, self.n_f, min(TILE, self.own_rows)),
            out_shape=[out] * self.n_f,
            in_specs=[smem()] + [vmem()] * (3 + self.n_f) + [anywhere()] * len(after),
            out_specs=[vmem()] * self.n_f,
            scratch_shapes=[scratch, scratch],
            compiler_params=params(OTHER_MIB),
            cost_estimate=cost(WEIGHT, BYTES),
            name="window",
        )(self.where, self.limits[chunk], *self.tables, *blocks, *after)


class Chain:
    def __init__(self, plan, chunk, vector):
        self.plan, self.chunk, self.wave = plan, chunk, None
        self.vector, self.done, self.minus = vector, 0, None
        self.todo = self.theta()

    def theta(self):
        return [self.far, self.near] + [self.add] * self.plan.bits + [self.split, self.window, self.assemble]

    def step(self, after):
        return self.todo.pop(0)(after)

    def sign(self):
        return 1 if self.done % 2 == 0 else -1

    def far(self, after):
        out = self.plan.terms(self.vector, self.plan.far, self.sign(), after)
        self.arriving = self.plan.to_core(out)
        return [out]

    def near(self, after):
        out = self.plan.terms(self.vector, self.plan.near, self.sign(), after)
        self.addends, self.half = [out, self.arriving], self.plan.n_chip
        return [out]

    def add(self, after):
        plan = self.plan
        self.half //= 2
        send = plan.add(self.addends, self.half, after)
        self.addends.append(plan.to_chip(send, len(self.addends) - 2))
        return [send]

    def split(self, after):
        blocks = self.plan.split(self.addends, after)
        self.blocks = self.plan.exchange(blocks)
        return [blocks[0]]

    def window(self, after):
        blocks = self.plan.window(self.blocks, self.chunk, after)
        self.blocks = self.plan.exchange(blocks)
        return [blocks[0]]

    def assemble(self, after):
        self.done += 1
        wave = self.wave if self.done % 2 == 0 and self.done < 2 * ITERS else None
        self.vector = self.plan.assemble(self.blocks, wave, after)
        if self.done == 2 * ITERS - 1:
            self.minus = self.vector
        self.todo = self.theta()
        return [self.vector]


def local(reflection, direct_wave, first_arrival):
    plan = Plan(reflection, direct_wave)
    plus = plan.pack(direct_wave)
    chains = [Chain(plan, i, plus[i]) for i in range(plan.chunks)]
    after = []
    for step in range(2 * ITERS):
        for i in ORDER if step else START:
            after = chains[int(i)].step(after)
        if step == 0:
            after = plan.make_limits(first_arrival, after)
        if step == 1:
            waves = plan.waves(direct_wave, after)
            after = waves[:1]
            for chain, wave in zip(chains, waves):
                chain.wave = wave
        for _ in range(1 + plan.bits):
            for chain in chains:
                after = chain.step(after)
    for chain in chains:
        after = chain.step(after)
    return plan.unpack([c.minus for c in chains]), plan.unpack([c.vector for c in chains], direct_wave)


def solution(mesh):
    in_specs = (P(None, "freq", None, "src"), P("src", "freq", None), P(("src", "freq"), None))
    out_specs = (P("src", "freq", None), P("src", "freq", None))
    return jax.shard_map(local, mesh=mesh, in_specs=in_specs, out_specs=out_specs, check_vma=False)
```
